128 devices in a mesh: seq: 32 (over z, y, core), kvh: 4 (over x).
Axes of the slice: x: 4, y: 4, z: 4, core: 2. Of those that a mesh axis runs over, the one named last changes fastest.
Arguments:
- queries: bfloat16 [16384, 4096], P('seq', 'kvh'), as said below
- span_kv: bfloat16 [2, 16384, 1024], P(None, 'seq', 'kvh'), as said below
- cache: bfloat16 [2, 262144, 1024], P(None, 'seq', 'kvh'), as said below
- block_group: int32 [8, 128, 3], P('kvh', 'seq'), may hold values from 0 to 31, all different within a row; in each aligned block of 4 rows (0 to 3, 4 to 7, ..., all dimensions but the last counted through in order) no two rows name the same one
- block_within: int32 [8, 128, 3], P('kvh', 'seq'), may hold values from 0 to 14
- span_start: int32 [1], replicated, may hold values from 261633 to 262144
- out_weight: bfloat16 [4096, 4096], P('kvh'), may hold values from -0.09375 to 0.09375
Outputs:
- mixed: float32 [16384, 4096], P(('seq', 'kvh'))
The draws below stay inside these ranges and needn't reach their ends.
Inputs may be any that keep to these rules, and one draw needn't show every extreme that they name: `block_group`: for each key-value head, the 4 tiles of one seq index (aligned blocks of 4 tiles) name one value at most 1 times, a bound that some block reaches; the 3 values of one tile and head differ. `block_within`: A chosen block is never the cache's last block. `queries`: of order one. `span_kv`: keys of order a few units, values of order one. `cache`: keys of order a few units, values of order one; slots from span_start on hold stale entries.
All inputs are finite; a program needn't handle non-finite values.
Results may differ from the reference program's by a relative error of at most 0.006.
Values may be sent and summed in bfloat16 or wider, within the bound.
No kernel may reach another device: no remote copies, remote signals or barrier semaphores. Data moves between devices by JAX's collectives and lax.ppermute only.
A program may use at most 192 MiB of HBM per device.

```python
import math
import jax
import jax.numpy as jnp
import numpy as np
from jax import lax

D = 4096
KVH = 8
HD = 128
GROUP = 4
H = 32
TILE = 128
BLOCK = 512
TOPK = 3
QT_DEV = 4
BLK_DEV = 16
CAP = 1
TILES = 128
SPAN = 16384
CACHE_TOK = 262144
N_SEQ = 32


def shared_keys(key):
    base = 2.5 * jax.random.truncated_normal(jax.random.fold_in(key, 71), -3.2, 3.2, (SPAN, KVH * HD), jnp.float32)
    return base


def draw_span_kv(key, part):
    key_rows = shared_keys(key)
    key = jax.random.fold_in(key, 5)
    value_rows = jax.random.truncated_normal(key, -4.0, 4.0, (SPAN, KVH * HD), jnp.float32)
    return jnp.stack([key_rows, value_rows]).astype(jnp.bfloat16)


def draw_queries(key, part):
    own_key = jax.random.fold_in(key, 6)
    query_rows = 1.2 * jax.random.truncated_normal(own_key, -4.0, 4.0, (SPAN, H * HD), jnp.float32)
    return query_rows.astype(jnp.bfloat16)


def draw_cache(key, part):
    key = jax.random.fold_in(key, 9)
    first_key, second_key = jax.random.split(key)
    key_rows = 2.5 * jax.random.truncated_normal(first_key, -3.2, 3.2, (CACHE_TOK, KVH * HD), jnp.float32)
    value_rows = jax.random.truncated_normal(second_key, -4.0, 4.0, (CACHE_TOK, KVH * HD), jnp.float32)
    return jnp.stack([key_rows, value_rows]).astype(jnp.bfloat16)


def with_ends(values, key, low, high):
    longest = values.shape.index(max(values.shape))
    spots = []
    for shift in (0, 1):
        where = [jax.random.randint(jax.random.fold_in(key, axis), (), 0, length) for axis, length in enumerate(values.shape)]
        where[longest] = (where[longest] + shift) % values.shape[longest]
        spots.append(tuple(where))
    return values.at[spots[0]].set(low).at[spots[1]].set(high)


def levels(key, extent, pieces, low, top_value):
    gain = 1.0
    for axis_at, parts in pieces:
        heights = jax.random.uniform(jax.random.fold_in(jax.random.fold_in(key, 6), axis_at), (parts,), jnp.float32, low / len(pieces), top_value / len(pieces))
        gain = gain * jnp.repeat(jnp.exp(heights), extent[axis_at] // parts).reshape((-1,) + (1,) * (len(extent) - 1 - axis_at))
    return gain


def assign_block(key, own, number, rows, count, top, limit, lean):
    ranking = jax.random.permutation(key, count)
    packed, usual = load_shares(count, rows * top, limit, lean, True), load_shares(count, rows * top, limit, lean, False)
    places = jnp.arange(count)

    def named(tallies, rotation):
        used = int((tallies > 0).sum())
        fixed = max(1, used // 4)
        passed = fixed + (places - fixed + rotation * (used - fixed)) % max(1, count - fixed)
        return jnp.zeros((count,), jnp.int32).at[ranking[jnp.where(places < fixed, places, passed)]].set(jnp.asarray(tallies, jnp.int32))

    tallies = jnp.where(number % 4 == 0, named(packed, number // 4), named(usual, number - number // 4 - 1))
    mixed = jax.random.permutation(jax.random.fold_in(own, 3), count)
    giver, receiver = mixed[0:count // 2 * 2:2], mixed[1:count // 2 * 2:2]
    slack = jnp.minimum(tallies[giver] - 1, limit - tallies[receiver]) // 2
    slack = jnp.where((giver == ranking[0]) | (receiver == ranking[0]) | (tallies[receiver] == 0), 0, jnp.maximum(slack, 0))
    passed = jax.random.randint(jax.random.fold_in(own, 4), (count // 2,), 0, 1 << 20) % (slack + 1)
    tallies = tallies.at[giver].add(-passed).at[receiver].add(passed)
    items = jnp.searchsorted(jnp.cumsum(tallies), jnp.arange(rows * top), side="right").astype(jnp.int32)
    grid = items.reshape(top, rows).T
    grid = grid[jax.random.permutation(jax.random.fold_in(own, 1), rows)]
    rotation = jax.random.randint(jax.random.fold_in(own, 2), (rows, 1), 0, top)
    return jnp.take_along_axis(grid, (jnp.arange(top)[None, :] + rotation) % top, axis=1)


def load_shares(number_of, total, bound, skew, full):
    weights = [(1 << 20) // math.isqrt(standing ** skew) + 1 for standing in range(1, number_of + 1)]
    largest = bound if full else min(bound, max(-(-total // number_of), total * weights[0] // sum(weights)))
    least = 1 if total - largest >= number_of - 1 else 0
    given, spare = [largest] + [least] * (number_of - 1), total - largest - least * (number_of - 1)
    while spare > 0:
        free = [i for i in range(1, number_of) if given[i] < largest] or [i for i in range(1, number_of) if given[i] < bound]
        pool, budget = sum([weights[i] for i in free]), spare
        for i in free:
            extra = min(bound - given[i], max(1, budget * weights[i] // pool), spare)
            given[i] = given[i] + extra
            spare = spare - extra
    return np.array(given)


def normal_values(stream_key, extent, scale, most, cuts=(), kind=jnp.bfloat16):
    values = scale * jax.random.normal(stream_key, extent, jnp.float32)
    if cuts:
        values = values * levels(stream_key, extent, cuts, -0.22, 0.18)
    return jnp.clip(values, -most, most).astype(kind)


def setup_inputs(seed: int = 0) -> dict:
    keys = jax.random.split(jax.random.key(seed), 8)
    queries = draw_queries(jax.random.fold_in(keys[7], 71), 0)
    span_kv = draw_span_kv(jax.random.fold_in(keys[7], 71), 0)
    cache = draw_cache(jax.random.fold_in(keys[7], 71), 0)
    block_group_keys = jax.random.split(jax.random.fold_in(keys[3], 1), KVH * TILES // QT_DEV)
    block_group_turns = jax.random.permutation(jax.random.fold_in(keys[3], 3), KVH * TILES // QT_DEV)
    block_group = jax.vmap(lambda own, number: assign_block(jax.random.fold_in(keys[3], 2), own, number, QT_DEV, N_SEQ, TOPK, CAP, 2))(block_group_keys, block_group_turns).reshape((KVH, TILES, TOPK))
    block_within = with_ends(jax.random.randint(keys[4], (KVH, TILES, TOPK), 0, BLK_DEV - 1), jax.random.fold_in(keys[4], 1), 0, (BLK_DEV - 1) - 1).astype(jnp.int32)
    span_start = jax.random.randint(keys[5], (1,), CACHE_TOK - BLOCK + 1, CACHE_TOK + 1).astype(jnp.int32)
    out_weight = normal_values(keys[6], (H * HD, D), (H * HD) ** -0.5, 0.09375, ((0, 4),))
    return dict(queries=queries, span_kv=span_kv, cache=cache, block_group=block_group, block_within=block_within, span_start=span_start, out_weight=out_weight)


def partial_attend(query_rows, key_rows, value_rows, allowed):
    scale = 1.0 / (query_rows.shape[-1] ** 0.5)
    scores = jnp.dot(query_rows, key_rows.T, preferred_element_type=jnp.float32) * scale
    scores = jnp.where(allowed, scores, jnp.float32(-1e30))
    row_max = jnp.max(scores, axis=1)
    weights = jnp.exp(scores - row_max[:, None])
    row_total = jnp.sum(weights, axis=1)
    weighted = jnp.dot(weights.astype(jnp.bfloat16), value_rows, preferred_element_type=jnp.float32)
    return row_max, row_total, weighted


def reference(queries, span_kv, cache, block_group, block_within, span_start, out_weight):
    tiles_per = BLOCK // TILE
    own_blocks = span_kv.reshape(2, SPAN // BLOCK, BLOCK, KVH, HD)
    cache_blocks = cache.reshape(2, CACHE_TOK // BLOCK, BLOCK, KVH, HD)
    query_tiles = queries.reshape(TILES, TILE, KVH, GROUP, HD)
    first_pos = span_start[0]
    row_count = GROUP * TILE
    token_ids = jnp.arange(row_count, dtype=jnp.int32) % TILE
    key_ids = jnp.arange(BLOCK, dtype=jnp.int32)
    tail_ok = (CACHE_TOK - BLOCK + key_ids) < first_pos

    def attend_tile(element):
        head_id = element // TILES
        tile_id = element % TILES
        picked_tile = lax.dynamic_index_in_dim(query_tiles, tile_id, 0, False)
        picked_head = lax.dynamic_index_in_dim(picked_tile, head_id, 1, False)
        query_rows = picked_head.transpose(1, 0, 2).reshape(row_count, HD)
        own_kv = own_blocks[:, tile_id // tiles_per, :, head_id, :]
        chosen_ids = block_group[head_id, tile_id] * BLK_DEV + block_within[head_id, tile_id]
        chosen_kv = cache_blocks[:, chosen_ids, :, head_id, :]
        tail_kv = cache_blocks[:, CACHE_TOK // BLOCK - 1, :, head_id, :]
        key_rows = jnp.concatenate([own_kv[0], chosen_kv[:, 0].reshape(TOPK * BLOCK, HD), tail_kv[0]], axis=0)
        value_rows = jnp.concatenate([own_kv[1], chosen_kv[:, 1].reshape(TOPK * BLOCK, HD), tail_kv[1]], axis=0)
        base = (tile_id % tiles_per) * TILE
        own_ok = key_ids[None, :] <= (base + token_ids)[:, None]
        allowed = jnp.concatenate([own_ok, jnp.ones((row_count, TOPK * BLOCK), dtype=bool), jnp.broadcast_to(tail_ok[None, :], (row_count, BLOCK))], axis=1)
        row_max, row_total, weighted = partial_attend(query_rows, key_rows, value_rows, allowed)
        result = (weighted / row_total[:, None]).astype(jnp.bfloat16)
        return result.reshape(GROUP, TILE, HD).transpose(1, 0, 2).reshape(TILE, GROUP * HD)

    results = lax.map(attend_tile, jnp.arange(KVH * TILES, dtype=jnp.int32))
    attended = results.reshape(KVH, TILES, TILE, GROUP * HD).transpose(1, 2, 0, 3).reshape(SPAN, H * HD)
    return jnp.dot(attended, out_weight, preferred_element_type=jnp.float32)
```

```python
import functools
import math

import jax
import jax.numpy as jnp
from jax import lax
from jax.experimental import pallas as pl
from jax.experimental.pallas import tpu as pltpu
from jax.sharding import PartitionSpec as P

TILE = 128
BLOCK = 512
HD = 128
GROUP = 4
ROWS = GROUP * TILE
PAYLOAD = ROWS + 16
VMEM_LIMIT = 16 * 1024 * 1024
COEF = math.log2(math.e) / math.sqrt(HD)


SMALL = pl.CostEstimate(flops=1 << 20, bytes_accessed=1 << 16, transcendentals=0)


def params():
    return pltpu.CompilerParams(vmem_limit_bytes=VMEM_LIMIT)


def pinned(*arrays):
    return [pltpu.with_memory_space_constraint(x, pltpu.HBM) for x in arrays]


def position(me):
    return me >> 3, (me >> 1) & 3, me & 1


def device(z, y, c):
    return ((z & 3) << 3) | ((y & 3) << 1) | c


def moved(h, place, first, second, flip):
    z, y, c = place
    if h == 0:
        return device(z + second, y + first, c ^ flip)
    return device(z + first, y + second, c ^ flip)


def code_at(codes, h, asker, owner):
    return codes[(asker * 2 + h) * 32 + owner]


def eye_mask():
    a = lax.broadcasted_iota(jnp.int32, (TILE, TILE), 0)
    b = lax.broadcasted_iota(jnp.int32, (TILE, TILE), 1)
    return a == b


def softmax_part(q, k, values_ones, allowed=None):
    s = lax.dot_general(q, k, (((1,), (1,)), ((), ())), preferred_element_type=jnp.float32)
    if allowed is not None:
        s = jnp.where(allowed, s, jnp.float32(-1e30))
    m = jnp.max(s, axis=1, keepdims=True)
    p = jnp.exp2((s - m) * COEF).astype(jnp.bfloat16)
    both = jnp.dot(p, values_ones, preferred_element_type=jnp.float32)
    total = both[:, HD:]
    return both[:, :HD] / total, m * COEF + jnp.log2(total)


def with_ones(v):
    return jnp.concatenate([v, jnp.ones_like(v)], axis=1)


def to_row(column, eye):
    return jnp.sum(jnp.where(eye, column, 0.0), axis=0, keepdims=True)


def to_column(row, eye):
    return jnp.sum(jnp.where(eye, row, 0.0), axis=1, keepdims=True)


def split_kernel(q_ref, out0, out1):
    for h, out in enumerate((out0, out1)):
        for g in range(GROUP):
            out[0, pl.ds(g * TILE, TILE), :] = q_ref[:, (h * GROUP + g) * HD : (h * GROUP + g + 1) * HD]


def split(queries):
    shape = pltpu.HBM((4, ROWS, HD), jnp.bfloat16)
    return pl.pallas_call(
        split_kernel,
        grid=(4,),
        in_specs=[pl.BlockSpec((TILE, queries.shape[1]), lambda t: (t, 0))],
        out_specs=[pl.BlockSpec((1, ROWS, HD), lambda t: (t, 0, 0))] * 2,
        out_shape=[shape, shape],
        compiler_params=params(),
        cost_estimate=SMALL,
        name="split",
    )(*pinned(queries))


def pack_kernel(codes, me, *refs):
    held, outs, sem = refs[:10], refs[10:18], refs[18]
    place = position(me[0])

    def each(act):
        for h in range(2):
            own, one, three, low, high = held[h * 5 : h * 5 + 5]
            for e in range(4):
                for d in range(4):
                    asker = moved(h, place, -d, 0, 0)
                    for f in range(2):
                        code = code_at(codes, h, asker, moved(h, place, 0, e, f))
                        tile = jnp.maximum(code, 0) >> 4
                        n = ((h * 4 + e) * 4 + d) * 2 + f
                        target = outs[h * 4 + e].at[f, d]
                        if d != 2:
                            source = (own, one, None, three)[d]

                            @pl.when(code >= 0)
                            def _():
                                act(pltpu.make_async_copy(source.at[tile], target, sem.at[n]))

                        else:

                            @pl.when((code >= 0) & (tile < 2))
                            def _():
                                act(pltpu.make_async_copy(low.at[tile & 1], target, sem.at[n]))

                            @pl.when((code >= 0) & (tile >= 2))
                            def _():
                                act(pltpu.make_async_copy(high.at[tile & 1], target, sem.at[n]))

    each(lambda copy: copy.start())
    each(lambda copy: copy.wait())


def pack(codes, me, held):
    shape = pltpu.HBM((2, 4, ROWS, HD), jnp.bfloat16)

    def whole(x):
        return pl.BlockSpec(x.shape, lambda i, c, m: (0, 0, 0))

    outs = pl.pallas_call(
        pack_kernel,
        grid_spec=pltpu.PrefetchScalarGridSpec(
            num_scalar_prefetch=2,
            grid=(1,),
            in_specs=[whole(x) for x in held],
            out_specs=[pl.BlockSpec(memory_space=pltpu.HBM)] * 8,
            scratch_shapes=[pltpu.SemaphoreType.DMA((64,))],
        ),
        out_shape=[shape] * 8,
        compiler_params=params(),
        cost_estimate=SMALL,
        name="pack",
    )(codes, me, *pinned(*held))
    return outs[:4], outs[4:]


ITEMS = [(h, f) for h in range(2) for f in range(2)]


def lse_parts(lse):
    first = lse.astype(jnp.bfloat16).astype(jnp.float32)
    rest = lse - first
    second = rest.astype(jnp.bfloat16).astype(jnp.float32)
    third = rest - second
    parts = jnp.concatenate([first, second, third, jnp.zeros_like(third)], axis=0)
    return parts.astype(jnp.bfloat16)


def lse_rows(parts):
    parts = parts.astype(jnp.float32)
    return parts[0:4] + parts[4:8] + parts[8:12]


def slot_code(e, item, d, codes, me):
    h, f = item
    asker = moved(h, position(me[0]), -d, -e, 0)
    return code_at(codes, h, asker, me[0] ^ f)


def slot_kernel(e, codes, me, *refs):
    n = len(ITEMS)
    qs, ks, vs, outs = refs[:2], refs[2 : 2 + n], refs[2 + n : 2 + 2 * n], refs[2 + 2 * n :]
    d = pl.program_id(0)
    for i, item in enumerate(ITEMS):
        h, f = item

        @pl.when(slot_code(e, item, d, codes, me) >= 0)
        def _():
            eye = eye_mask()
            k = ks[i][0]
            vo = with_ones(vs[i][0])
            rows = []
            for g in range(GROUP):
                at = pl.ds(g * TILE, TILE)
                o, lse = softmax_part(qs[h][f, 0, at, :], k, vo)
                outs[h][f, 0, at, :] = o.astype(jnp.bfloat16)
                rows.append(to_row(lse, eye))
            outs[h][f, 0, pl.ds(ROWS, 16), :] = lse_parts(jnp.concatenate(rows, axis=0))


def attend_slots(e, codes, me, arrays, caches):
    n = len(ITEMS)

    def block(which, item):
        def index(d, codes, me):
            return which, jnp.maximum(slot_code(e, item, d, codes, me), 0) & 15, item[0]

        return pl.BlockSpec((1, BLOCK, HD), index)

    return pl.pallas_call(
        functools.partial(slot_kernel, e),
        grid_spec=pltpu.PrefetchScalarGridSpec(
            num_scalar_prefetch=2,
            grid=(4,),
            in_specs=[pl.BlockSpec((2, 1, ROWS, HD), lambda d, c, m: (0, d, 0, 0))] * 2
            + [block(0, item) for item in ITEMS]
            + [block(1, item) for item in ITEMS],
            out_specs=[pl.BlockSpec((2, 1, PAYLOAD, HD), lambda d, c, m: (0, d, 0, 0))] * 2,
        ),
        out_shape=[pltpu.HBM((2, 4, PAYLOAD, HD), jnp.bfloat16)] * 2,
        compiler_params=params(),
        cost_estimate=SMALL,
        name="slots",
    )(codes, me, *pinned(*arrays), *pinned(*([caches[f] for _, f in ITEMS] * 2)))


def local_kernel(start, q_ref, own_ref, tailk_ref, tailv_ref, o_ref, lse_ref, *, tail_base):
    t = pl.program_id(1)
    eye = eye_mask()
    k = jnp.concatenate([own_ref[0], tailk_ref[...]], axis=0)
    vo = with_ones(jnp.concatenate([own_ref[1], tailv_ref[...]], axis=0))
    key = lax.broadcasted_iota(jnp.int32, (TILE, 2 * BLOCK), 1)
    row = lax.broadcasted_iota(jnp.int32, (TILE, 2 * BLOCK), 0)
    limit = jnp.where(key < BLOCK, t * TILE + row + 1, start[0] - tail_base + 2 * BLOCK)
    allowed = key < limit
    for g in range(GROUP):
        o, lse = softmax_part(q_ref[:, g * HD : (g + 1) * HD], k, vo, allowed)
        o_ref[0, 0, g] = o
        lse_ref[0, 0, pl.ds(g, 1), :] = to_row(lse, eye)


def attend_local(start, queries, span_kv, tail, tail_base):
    one = pl.BlockSpec((BLOCK, HD), lambda h, t, s: (0, h))
    kv = pl.BlockSpec((2, BLOCK, HD), lambda h, t, s: (0, 0, h))
    return pl.pallas_call(
        functools.partial(local_kernel, tail_base=tail_base),
        grid_spec=pltpu.PrefetchScalarGridSpec(
            num_scalar_prefetch=1,
            grid=(2, 4),
            in_specs=[pl.BlockSpec((TILE, GROUP * HD), lambda h, t, s: (t, h)), kv, one, one],
            out_specs=[
                pl.BlockSpec((1, 1, GROUP, TILE, HD), lambda h, t, s: (h, t, 0, 0, 0)),
                pl.BlockSpec((1, 1, 8, TILE), lambda h, t, s: (h, t, 0, 0)),
            ],
        ),
        out_shape=[
            pltpu.HBM((2, 4, GROUP, TILE, HD), jnp.float32),
            pltpu.HBM((2, 4, 8, TILE), jnp.float32),
        ],
        compiler_params=params(),
        cost_estimate=SMALL,
        name="local",
    )(start, *pinned(queries, span_kv, *tail))


def ring_kernel(h, codes, me, *refs):
    slots, outs = refs[:4], refs[4:8]
    sums, lses, packed, sem = refs[8:]
    d = pl.program_id(0)
    place = position(me[0])
    asker = moved(h, place, -d, 0, 0)
    eye = eye_mask()
    sums[...] = jnp.zeros_like(sums)
    lses[...] = jnp.full(lses.shape, -1e30, jnp.float32)
    for e in range(4):
        for f in range(2):
            code = code_at(codes, h, asker, moved(h, place, 0, e, f))
            ref = slots[e].at[f]

            @pl.when(code >= 0)
            def _():
                t = jnp.maximum(code, 0) >> 4
                old = lses[t, 0:4]
                new = lse_rows(ref[0, pl.ds(ROWS, 16), :])
                top = jnp.maximum(old, new)
                weight_old = jnp.exp2(old - top)
                weight_new = jnp.exp2(new - top)
                total = weight_old + weight_new
                lses[t, 0:4] = top + jnp.log2(total)
                weight_old = weight_old / total
                weight_new = weight_new / total
                for g in range(GROUP):
                    at = pl.ds(g * TILE, TILE)
                    sums[t, at, :] = to_column(weight_old[g : g + 1], eye) * sums[t, at, :] + to_column(
                        weight_new[g : g + 1], eye
                    ) * ref[0, at, :].astype(jnp.float32)

    for t in range(4):
        packed[d & 1, t, pl.ds(0, ROWS), :] = sums[t].astype(jnp.bfloat16)
        packed[d & 1, t, pl.ds(ROWS, 16), :] = lse_parts(lses[t, 0:4])
    copies = [pltpu.make_async_copy(packed.at[n % 2], outs[n], sem.at[n % 2]) for n in range(4)]
    for n in range(4):

        @pl.when(d == n)
        def _():
            copies[n].start()
            if n > 0:
                copies[n - 1].wait()
            if n == 3:
                copies[n].wait()


def merge_ring(h, codes, me, slots):
    return pl.pallas_call(
        functools.partial(ring_kernel, h),
        grid_spec=pltpu.PrefetchScalarGridSpec(
            num_scalar_prefetch=2,
            grid=(4,),
            in_specs=[pl.BlockSpec((2, 1, PAYLOAD, HD), lambda d, c, m: (0, d, 0, 0))] * 4,
            out_specs=[pl.BlockSpec(memory_space=pltpu.HBM)] * 4,
            scratch_shapes=[
                pltpu.VMEM((4, ROWS, HD), jnp.float32),
                pltpu.VMEM((4, 8, HD), jnp.float32),
                pltpu.VMEM((2, 4, PAYLOAD, HD), jnp.bfloat16),
                pltpu.SemaphoreType.DMA((2,)),
            ],
        ),
        out_shape=[pltpu.HBM((4, PAYLOAD, HD), jnp.bfloat16)] * 4,
        compiler_params=params(),
        cost_estimate=SMALL,
        name="ring",
    )(codes, me, *pinned(*slots))


def merge_kernel(own_ref, lse_ref, *refs):
    parts, o_ref = refs[:8], refs[8]
    eye = eye_mask()
    for h in range(2):
        arrived = parts[4 * h : 4 * h + 4]
        rows = [lse_ref[h, 0, 0:4, :]] + [lse_rows(ref[0, pl.ds(ROWS, 16), :]) for ref in arrived]
        top = functools.reduce(jnp.maximum, rows)
        weights = [jnp.exp2(x - top) for x in rows]
        total = functools.reduce(jnp.add, weights)
        weights = [w / total for w in weights]
        for g in range(GROUP):
            sums = [own_ref[h, 0, g]] + [ref[0, pl.ds(g * TILE, TILE), :].astype(jnp.float32) for ref in arrived]
            terms = [to_column(w[g : g + 1], eye) * s for w, s in zip(weights, sums)]
            at = (h * GROUP + g) * HD
            o_ref[0, :, at : at + HD] = functools.reduce(jnp.add, terms).astype(jnp.bfloat16)


def merge(own, lse, parts):
    part = pl.BlockSpec((1, PAYLOAD, HD), lambda t: (t, 0, 0))
    return pl.pallas_call(
        merge_kernel,
        grid=(4,),
        in_specs=[
            pl.BlockSpec((2, 1, GROUP, TILE, HD), lambda t: (0, t, 0, 0, 0)),
            pl.BlockSpec((2, 1, 8, TILE), lambda t: (0, t, 0, 0)),
        ]
        + [part] * 8,
        out_specs=pl.BlockSpec((1, TILE, 2 * GROUP * HD), lambda t: (t, 0, 0)),
        out_shape=jax.ShapeDtypeStruct((4, TILE, 2 * GROUP * HD), jnp.bfloat16),
        compiler_params=params(),
        cost_estimate=SMALL,
        name="merge",
    )(*pinned(own, lse, *parts[0], *parts[1]))


def shift(x, h, first, second, flip=0):
    pairs = [(i, moved(h, position(i), first, second, flip)) for i in range(32)]
    return lax.ppermute(x, "seq", pairs)


def tail_step(tail, step):
    if step == 0:
        pairs = [(device(3, 3, c), device(3, 0, c)) for c in range(2)]
    elif step == 1:
        pairs = [(device(3, a, c), device(3, b, c)) for a, b in ((3, 2), (0, 1)) for c in range(2)]
    elif step == 2:
        pairs = [(device(3, y, c), device(0, y, c)) for y in range(4) for c in range(2)]
    else:
        pairs = [(device(a, y, c), device(b, y, c)) for a, b in ((3, 2), (0, 1)) for y in range(4) for c in range(2)]
    return tail + lax.ppermute(tail, "seq", pairs)


def swap(x):
    return shift(x, 0, 0, 0, 1)


def all_to_all(x, axis):
    return lax.all_to_all(x, axis, split_axis=0, concat_axis=0, tiled=True)


def shards(queries, span_kv, cache, block_group, block_within, span_start, out_weight):
    seq_count = lax.axis_size("seq")
    me = lax.axis_index("seq")
    core = me & 1
    cache_len = cache.shape[1] * seq_count

    hits = block_group[:, None] == jnp.arange(seq_count, dtype=jnp.int32)[None, :, None, None]
    tiles = jnp.arange(4, dtype=jnp.int32)[None, None, :, None]
    code = jnp.sum(jnp.where(hits, block_within[:, None] + tiles * 16 + 1, 0), axis=(2, 3)) - 1
    codes = all_to_all(jnp.broadcast_to(code.reshape(1, -1), (seq_count, 2 * seq_count)), "seq").reshape(-1)
    place = me.reshape(1)

    barrier = lax.optimization_barrier
    own_tiles = split(queries)
    one = [shift(own_tiles[h], h, 1, 0) for h in range(2)]
    three = [shift(own_tiles[h], h, 3, 0) for h in range(2)]
    partner = swap(cache)
    codes, one, three, partner = barrier((codes, one, three, partner))
    low = [shift(one[h][:2], h, 1, 0) for h in range(2)]
    high = [shift(three[h][2:], h, 3, 0) for h in range(2)]
    last = jnp.where(core == 0, partner[0, -BLOCK:], cache[1, -BLOCK:])
    tail = tail_step(jnp.where(me >= seq_count - 2, last, jnp.zeros_like(last)), 0)
    out_weight, tail = barrier((out_weight, tail))
    half = lax.dynamic_slice_in_dim(out_weight, core * 512, 512, 0)
    mine = lax.all_gather(half, "kvh", axis=0, tiled=True)
    low, high, tail, half = barrier((low, high, tail, half))

    def attend(e, arrays):
        return attend_slots(e, codes, place, arrays, (cache, partner))

    packed = pack(codes, place, [x for h in range(2) for x in (own_tiles[h], one[h], three[h], low[h], high[h])])
    near = [[shift(packed[h][e], h, 0, e) for h in range(2)] for e in (1, 3)]
    tail = tail_step(tail, 1)
    back0 = attend(0, [packed[h][0] for h in range(2)])
    far = [packed[h][2] for h in range(2)]
    near, far, tail, back0 = barrier((near, far, tail, back0))
    far = [shift(far[h], h, 0, 2) for h in range(2)]
    tail = tail_step(tail, 2)
    out1 = attend(1, near[0])
    out3 = attend(3, near[1])
    far, tail, out1, out3 = barrier((far, tail, out1, out3))
    back1 = [shift(out1[h], h, 0, -1) for h in range(2)]
    back3 = [shift(out3[h], h, 0, -3) for h in range(2)]
    tail = tail_step(tail, 3)
    out2 = attend(2, far)
    back1, back3, tail, out2 = barrier((back1, back3, tail, out2))
    back2 = [shift(out2[h], h, 0, -2) for h in range(2)]
    other = swap(tail)
    tail = jnp.where(core == 0, tail, other), jnp.where(core == 0, other, tail)
    own, lse = attend_local(span_start, queries, span_kv, tail, cache_len)
    back1, back3, back2, own, lse = barrier((back1, back3, back2, own, lse))

    rings = [merge_ring(h, codes, place, (back0[h], back1[h], back2[h], back3[h])) for h in range(2)]
    parts = [[rings[h][0]] + [shift(rings[h][d], h, -d, 0) for d in (1, 3, 2)] for h in range(2)]
    parts, mine = barrier((parts, mine))
    rows = all_to_all(merge(own, lse, parts), "kvh")
    other = swap(mine)
    rows = [rows[:, :, h * 512 : h * 512 + 512] for h in range(2)]
    rows = [r.transpose(1, 0, 2).reshape(TILE, 2048) for r in rows]
    first = jnp.where(core == 0, rows[0], rows[1])
    second = jnp.where(core == 0, rows[1], rows[0])
    return jnp.dot(first, mine, preferred_element_type=jnp.float32) + jnp.dot(
        second, other, preferred_element_type=jnp.float32
    )


def solution(mesh):
    in_specs = (
        P("seq", "kvh"),
        P(None, "seq", "kvh"),
        P(None, "seq", "kvh"),
        P("kvh", "seq", None),
        P("kvh", "seq", None),
        P(),
        P("kvh", None),
    )
    out_specs = P(("seq", "kvh"), None)
    return jax.shard_map(shards, mesh=mesh, in_specs=in_specs, out_specs=out_specs, check_vma=False)
```

```python
import functools
import math

import jax
import jax.numpy as jnp
from jax import lax
from jax.experimental import pallas as pl
from jax.experimental.pallas import tpu as pltpu
from jax.sharding import PartitionSpec as P

TILE = 128
BLOCK = 512
HD = 128
GROUP = 4
ROWS = GROUP * TILE
PAYLOAD = ROWS + 16
VMEM_LIMIT = 16 * 1024 * 1024
COEF = math.log2(math.e) / math.sqrt(HD)


SMALL = pl.CostEstimate(flops=1 << 20, bytes_accessed=1 << 16, transcendentals=0)


def params():
    return pltpu.CompilerParams(vmem_limit_bytes=VMEM_LIMIT)


def pinned(*arrays):
    return [pltpu.with_memory_space_constraint(x, pltpu.HBM) for x in arrays]


def position(me):
    return me >> 3, (me >> 1) & 3, me & 1


def device(z, y, c):
    return ((z & 3) << 3) | ((y & 3) << 1) | c


def moved(h, place, first, second, flip):
    z, y, c = place
    if h == 0:
        return device(z + second, y + first, c ^ flip)
    return device(z + first, y + second, c ^ flip)


def code_at(codes, h, asker, owner):
    return codes[(asker * 2 + h) * 32 + owner]


def eye_mask():
    a = lax.broadcasted_iota(jnp.int32, (TILE, TILE), 0)
    b = lax.broadcasted_iota(jnp.int32, (TILE, TILE), 1)
    return a == b


def softmax_part(q, k, values_ones, allowed=None):
    s = lax.dot_general(q, k, (((1,), (1,)), ((), ())), preferred_element_type=jnp.float32)
    if allowed is not None:
        s = jnp.where(allowed, s, jnp.float32(-1e30))
    m = jnp.max(s, axis=1, keepdims=True)
    p = jnp.exp2((s - m) * COEF).astype(jnp.bfloat16)
    both = jnp.dot(p, values_ones, preferred_element_type=jnp.float32)
    total = both[:, HD:]
    return both[:, :HD] / total, m * COEF + jnp.log2(total)


def with_ones(v):
    return jnp.concatenate([v, jnp.ones_like(v)], axis=1)


def to_row(column, eye):
    return jnp.sum(jnp.where(eye, column, 0.0), axis=0, keepdims=True)


def to_column(row, eye):
    return jnp.sum(jnp.where(eye, row, 0.0), axis=1, keepdims=True)


def split_kernel(q_ref, out0, out1):
    for h, out in enumerate((out0, out1)):
        for g in range(GROUP):
            out[0, pl.ds(g * TILE, TILE), :] = q_ref[:, (h * GROUP + g) * HD : (h * GROUP + g + 1) * HD]


def split(queries):
    shape = pltpu.HBM((4, ROWS, HD), jnp.bfloat16)
    return pl.pallas_call(
        split_kernel,
        grid=(4,),
        in_specs=[pl.BlockSpec((TILE, queries.shape[1]), lambda t: (t, 0))],
        out_specs=[pl.BlockSpec((1, ROWS, HD), lambda t: (t, 0, 0))] * 2,
        out_shape=[shape, shape],
        compiler_params=params(),
        cost_estimate=SMALL,
        name="split",
    )(*pinned(queries))


def pack_kernel(codes, me, *refs):
    held, outs, sem = refs[:10], refs[10:18], refs[18]
    place = position(me[0])

    def each(act):
        for h in range(2):
            own, one, three, low, high = held[h * 5 : h * 5 + 5]
            for e in range(4):
                for d in range(4):
                    asker = moved(h, place, -d, 0, 0)
                    for f in range(2):
                        code = code_at(codes, h, asker, moved(h, place, 0, e, f))
                        tile = jnp.maximum(code, 0) >> 4
                        n = ((h * 4 + e) * 4 + d) * 2 + f
                        target = outs[h * 4 + e].at[f, d]
                        if d != 2:
                            source = (own, one, None, three)[d]

                            @pl.when(code >= 0)
                            def _():
                                act(pltpu.make_async_copy(source.at[tile], target, sem.at[n]))

                        else:

                            @pl.when((code >= 0) & (tile < 2))
                            def _():
                                act(pltpu.make_async_copy(low.at[tile & 1], target, sem.at[n]))

                            @pl.when((code >= 0) & (tile >= 2))
                            def _():
                                act(pltpu.make_async_copy(high.at[tile & 1], target, sem.at[n]))

    each(lambda copy: copy.start())
    each(lambda copy: copy.wait())


def pack(codes, me, held):
    shape = pltpu.HBM((2, 4, ROWS, HD), jnp.bfloat16)

    def whole(x):
        return pl.BlockSpec(x.shape, lambda i, c, m: (0, 0, 0))

    outs = pl.pallas_call(
        pack_kernel,
        grid_spec=pltpu.PrefetchScalarGridSpec(
            num_scalar_prefetch=2,
            grid=(1,),
            in_specs=[whole(x) for x in held],
            out_specs=[pl.BlockSpec(memory_space=pltpu.HBM)] * 8,
            scratch_shapes=[pltpu.SemaphoreType.DMA((64,))],
        ),
        out_shape=[shape] * 8,
        compiler_params=params(),
        cost_estimate=SMALL,
        name="pack",
    )(codes, me, *pinned(*held))
    return outs[:4], outs[4:]


def half_kernel(core, w_ref, o_ref):
    o_ref[...] = w_ref[...]


def half_rows(core, weights):
    rows, columns = weights.shape[0] // 8, weights.shape[1]
    return pl.pallas_call(
        half_kernel,
        grid_spec=pltpu.PrefetchScalarGridSpec(
            num_scalar_prefetch=1,
            grid=(4,),
            in_specs=[pl.BlockSpec((rows, columns), lambda i, c: (c[0] * 4 + i, 0))],
            out_specs=pl.BlockSpec((rows, columns), lambda i, c: (i, 0)),
        ),
        out_shape=pltpu.HBM((rows * 4, columns), weights.dtype),
        compiler_params=params(),
        cost_estimate=SMALL,
        name="half",
    )(core, *pinned(weights))


ITEMS = [(h, f) for h in range(2) for f in range(2)]


def lse_parts(lse):
    first = lse.astype(jnp.bfloat16).astype(jnp.float32)
    rest = lse - first
    second = rest.astype(jnp.bfloat16).astype(jnp.float32)
    third = rest - second
    parts = jnp.concatenate([first, second, third, jnp.zeros_like(third)], axis=0)
    return parts.astype(jnp.bfloat16)


def lse_rows(parts):
    parts = parts.astype(jnp.float32)
    return parts[0:4] + parts[4:8] + parts[8:12]


def slot_code(e, item, d, codes, me):
    h, f = item
    asker = moved(h, position(me[0]), -d, -e, 0)
    return code_at(codes, h, asker, me[0] ^ f)


def slot_kernel(*refs):
    n = len(ITEMS)
    refs = refs[2:]
    qs, ks, vs, outs = refs[:2], refs[2 : 2 + n], refs[2 + n : 2 + 2 * n], refs[2 + 2 * n :]
    eye = eye_mask()
    for i, (h, f) in enumerate(ITEMS):
        k = ks[i][0]
        vo = with_ones(vs[i][0])
        rows = []
        for g in range(GROUP):
            at = pl.ds(g * TILE, TILE)
            o, lse = softmax_part(qs[h][f, 0, at, :], k, vo)
            outs[h][f, 0, at, :] = o.astype(jnp.bfloat16)
            rows.append(to_row(lse, eye))
        outs[h][f, 0, pl.ds(ROWS, 16), :] = lse_parts(jnp.concatenate(rows, axis=0))


def attend_slots(e, codes, me, arrays, caches):
    n = len(ITEMS)

    def block(which, item):
        def index(d, codes, me):
            return which, jnp.maximum(slot_code(e, item, d, codes, me), 0) & 15, item[0]

        return pl.BlockSpec((1, BLOCK, HD), index)

    return pl.pallas_call(
        slot_kernel,
        grid_spec=pltpu.PrefetchScalarGridSpec(
            num_scalar_prefetch=2,
            grid=(4,),
            in_specs=[pl.BlockSpec((2, 1, ROWS, HD), lambda d, c, m: (0, d, 0, 0))] * 2
            + [block(0, item) for item in ITEMS]
            + [block(1, item) for item in ITEMS],
            out_specs=[pl.BlockSpec((2, 1, PAYLOAD, HD), lambda d, c, m: (0, d, 0, 0))] * 2,
        ),
        out_shape=[pltpu.HBM((2, 4, PAYLOAD, HD), jnp.bfloat16)] * 2,
        compiler_params=params(),
        cost_estimate=SMALL,
        name="slots",
    )(codes, me, *pinned(*arrays), *pinned(*([caches[f] for _, f in ITEMS] * 2)))


def local_kernel(start, q_ref, own_ref, tailk_ref, tailv_ref, o_ref, lse_ref, *, tail_base):
    t = pl.program_id(1)
    eye = eye_mask()
    k = jnp.concatenate([own_ref[0], tailk_ref[...]], axis=0)
    vo = with_ones(jnp.concatenate([own_ref[1], tailv_ref[...]], axis=0))
    key = lax.broadcasted_iota(jnp.int32, (TILE, 2 * BLOCK), 1)
    row = lax.broadcasted_iota(jnp.int32, (TILE, 2 * BLOCK), 0)
    limit = jnp.where(key < BLOCK, t * TILE + row + 1, start[0] - tail_base + 2 * BLOCK)
    allowed = key < limit
    for g in range(GROUP):
        o, lse = softmax_part(q_ref[:, g * HD : (g + 1) * HD], k, vo, allowed)
        o_ref[0, 0, g] = o
        lse_ref[0, 0, pl.ds(g, 1), :] = to_row(lse, eye)


def attend_local(start, queries, span_kv, tail, tail_base):
    one = pl.BlockSpec((BLOCK, HD), lambda h, t, s: (0, h))
    kv = pl.BlockSpec((2, BLOCK, HD), lambda h, t, s: (0, 0, h))
    return pl.pallas_call(
        functools.partial(local_kernel, tail_base=tail_base),
        grid_spec=pltpu.PrefetchScalarGridSpec(
            num_scalar_prefetch=1,
            grid=(2, 4),
            in_specs=[pl.BlockSpec((TILE, GROUP * HD), lambda h, t, s: (t, h)), kv, one, one],
            out_specs=[
                pl.BlockSpec((1, 1, GROUP, TILE, HD), lambda h, t, s: (h, t, 0, 0, 0)),
                pl.BlockSpec((1, 1, 8, TILE), lambda h, t, s: (h, t, 0, 0)),
            ],
        ),
        out_shape=[
            pltpu.HBM((2, 4, GROUP, TILE, HD), jnp.float32),
            pltpu.HBM((2, 4, 8, TILE), jnp.float32),
        ],
        compiler_params=params(),
        cost_estimate=SMALL,
        name="local",
    )(start, *pinned(queries, span_kv, *tail))


def ring_kernel(h, codes, me, *refs):
    slots, outs = refs[:4], refs[4:8]
    sums, lses, packed, sem = refs[8:]
    d = pl.program_id(0)
    place = position(me[0])
    asker = moved(h, place, -d, 0, 0)
    eye = eye_mask()
    sums[...] = jnp.zeros_like(sums)
    lses[...] = jnp.full(lses.shape, -1e30, jnp.float32)
    for e in range(4):
        for f in range(2):
            code = code_at(codes, h, asker, moved(h, place, 0, e, f))
            ref = slots[e].at[f]

            @pl.when(code >= 0)
            def _():
                t = jnp.maximum(code, 0) >> 4
                old = lses[t, 0:4]
                new = lse_rows(ref[0, pl.ds(ROWS, 16), :])
                top = jnp.maximum(old, new)
                weight_old = jnp.exp2(old - top)
                weight_new = jnp.exp2(new - top)
                total = weight_old + weight_new
                lses[t, 0:4] = top + jnp.log2(total)
                weight_old = weight_old / total
                weight_new = weight_new / total
                for g in range(GROUP):
                    at = pl.ds(g * TILE, TILE)
                    sums[t, at, :] = to_column(weight_old[g : g + 1], eye) * sums[t, at, :] + to_column(
                        weight_new[g : g + 1], eye
                    ) * ref[0, at, :].astype(jnp.float32)

    for t in range(4):
        packed[d & 1, t, pl.ds(0, ROWS), :] = sums[t].astype(jnp.bfloat16)
        packed[d & 1, t, pl.ds(ROWS, 16), :] = lse_parts(lses[t, 0:4])
    copies = [pltpu.make_async_copy(packed.at[n % 2], outs[n], sem.at[n % 2]) for n in range(4)]
    for n in range(4):

        @pl.when(d == n)
        def _():
            copies[n].start()
            if n > 0:
                copies[n - 1].wait()
            if n == 3:
                copies[n].wait()


def merge_ring(h, codes, me, slots):
    return pl.pallas_call(
        functools.partial(ring_kernel, h),
        grid_spec=pltpu.PrefetchScalarGridSpec(
            num_scalar_prefetch=2,
            grid=(4,),
            in_specs=[pl.BlockSpec((2, 1, PAYLOAD, HD), lambda d, c, m: (0, d, 0, 0))] * 4,
            out_specs=[pl.BlockSpec(memory_space=pltpu.HBM)] * 4,
            scratch_shapes=[
                pltpu.VMEM((4, ROWS, HD), jnp.float32),
                pltpu.VMEM((4, 8, HD), jnp.float32),
                pltpu.VMEM((2, 4, PAYLOAD, HD), jnp.bfloat16),
                pltpu.SemaphoreType.DMA((2,)),
            ],
        ),
        out_shape=[pltpu.HBM((4, PAYLOAD, HD), jnp.bfloat16)] * 4,
        compiler_params=params(),
        cost_estimate=SMALL,
        name="ring",
    )(codes, me, *pinned(*slots))


def merge_kernel(own_ref, lse_ref, *refs):
    parts, o_ref = refs[:8], refs[8]
    eye = eye_mask()
    for h in range(2):
        arrived = parts[4 * h : 4 * h + 4]
        rows = [lse_ref[h, 0, 0:4, :]] + [lse_rows(ref[0, pl.ds(ROWS, 16), :]) for ref in arrived]
        top = functools.reduce(jnp.maximum, rows)
        weights = [jnp.exp2(x - top) for x in rows]
        total = functools.reduce(jnp.add, weights)
        weights = [w / total for w in weights]
        for g in range(GROUP):
            sums = [own_ref[h, 0, g]] + [ref[0, pl.ds(g * TILE, TILE), :].astype(jnp.float32) for ref in arrived]
            terms = [to_column(w[g : g + 1], eye) * s for w, s in zip(weights, sums)]
            at = (h * GROUP + g) * HD
            o_ref[0, :, at : at + HD] = functools.reduce(jnp.add, terms).astype(jnp.bfloat16)


def merge(lane, own, lse, parts):
    part = pl.BlockSpec((1, PAYLOAD, HD), lambda d, k: ((k[0] + d) & 3, 0, 0))
    return pl.pallas_call(
        lambda lane, *refs: merge_kernel(*refs),
        grid_spec=pltpu.PrefetchScalarGridSpec(
            num_scalar_prefetch=1,
            grid=(4,),
            in_specs=[
                pl.BlockSpec((2, 1, GROUP, TILE, HD), lambda d, k: (0, (k[0] + d) & 3, 0, 0, 0)),
                pl.BlockSpec((2, 1, 8, TILE), lambda d, k: (0, (k[0] + d) & 3, 0, 0)),
            ]
            + [part] * 8,
            out_specs=pl.BlockSpec((1, TILE, 2 * GROUP * HD), lambda d, k: (d, 0, 0)),
        ),
        out_shape=jax.ShapeDtypeStruct((4, TILE, 2 * GROUP * HD), jnp.bfloat16),
        compiler_params=params(),
        cost_estimate=SMALL,
        name="merge",
    )(lane, *pinned(own, lse, *parts[0], *parts[1]))


def own_projection_kernel(x_ref, w_ref, o_ref):
    o_ref[...] = jnp.dot(x_ref[...], w_ref[...], preferred_element_type=jnp.float32)


def own_projection(x, weights):
    columns = 1024
    return pl.pallas_call(
        own_projection_kernel,
        grid=(weights.shape[1] // columns,),
        in_specs=[
            pl.BlockSpec(x.shape, lambda j: (0, 0)),
            pl.BlockSpec((weights.shape[0], columns), lambda j: (0, j)),
        ],
        out_specs=pl.BlockSpec((TILE, columns), lambda j: (0, j)),
        out_shape=pltpu.HBM((TILE, weights.shape[1]), jnp.float32),
        compiler_params=params(),
        cost_estimate=SMALL,
        name="own_projection",
    )(x, weights)


def projection_kernel(lane, core, sum_ref, *refs):
    rows, mine, other, o_ref = refs[:3], refs[3:6], refs[6:9], refs[9]
    total = sum_ref[...]
    half = rows[0].shape[1] // 2
    at = pl.multiple_of(core[0] * half, half)
    away = pl.multiple_of((1 - core[0]) * half, half)
    for d in range(3):
        total += jnp.dot(rows[d][:, pl.ds(at, half)], mine[d][0], preferred_element_type=jnp.float32)
        total += jnp.dot(rows[d][:, pl.ds(away, half)], other[d][0], preferred_element_type=jnp.float32)
    o_ref[...] = total


def projection(lane, core, total, rows, mine, other):
    columns = 512
    width = total.shape[1]

    def weight(d):
        return pl.BlockSpec((1, mine.shape[1], columns), lambda j, k, c: ((k[0] - d) & 3, 0, j))

    block = pl.BlockSpec((TILE, columns), lambda j, k, c: (0, j))
    return pl.pallas_call(
        projection_kernel,
        grid_spec=pltpu.PrefetchScalarGridSpec(
            num_scalar_prefetch=2,
            grid=(width // columns,),
            in_specs=[block]
            + [pl.BlockSpec(x.shape, lambda j, k, c: (0, 0)) for x in rows]
            + [weight(d) for d in (1, 2, 3)] * 2,
            out_specs=block,
        ),
        out_shape=jax.ShapeDtypeStruct(total.shape, jnp.float32),
        compiler_params=params(),
        cost_estimate=SMALL,
        name="projection",
    )(lane, core, *pinned(total, *rows), *([mine] * 3), *([other] * 3))


def shift(x, h, first, second, flip=0):
    pairs = [(i, moved(h, position(i), first, second, flip)) for i in range(32)]
    return lax.ppermute(x, "seq", pairs)


def tail_step(tail, step):
    if step == 0:
        pairs = [(device(3, 3, c), device(3, 0, c)) for c in range(2)]
    elif step == 1:
        pairs = [(device(3, a, c), device(3, b, c)) for a, b in ((3, 2), (0, 1)) for c in range(2)]
    elif step == 2:
        pairs = [(device(3, y, c), device(0, y, c)) for y in range(4) for c in range(2)]
    else:
        pairs = [(device(a, y, c), device(b, y, c)) for a, b in ((3, 2), (0, 1)) for y in range(4) for c in range(2)]
    return tail + lax.ppermute(tail, "seq", pairs)


def swap(x):
    return shift(x, 0, 0, 0, 1)


def all_to_all(x, axis):
    return lax.all_to_all(x, axis, split_axis=0, concat_axis=0, tiled=True)


def shards(queries, span_kv, cache, block_group, block_within, span_start, out_weight):
    seq_count = lax.axis_size("seq")
    me = lax.axis_index("seq")
    core = me & 1
    cache_len = cache.shape[1] * seq_count

    hits = block_group[:, None] == jnp.arange(seq_count, dtype=jnp.int32)[None, :, None, None]
    tiles = jnp.arange(4, dtype=jnp.int32)[None, None, :, None]
    code = jnp.sum(jnp.where(hits, block_within[:, None] + tiles * 16 + 1, 0), axis=(2, 3)) - 1
    codes = all_to_all(jnp.broadcast_to(code.reshape(1, -1), (seq_count, 2 * seq_count)), "seq").reshape(-1)
    place = me.reshape(1)

    barrier = lax.optimization_barrier
    own_tiles = split(queries)
    own_tiles, weights = barrier((own_tiles, out_weight))
    half = half_rows(core.reshape(1), weights)
    one = [shift(own_tiles[h], h, 1, 0) for h in range(2)]
    three = [shift(own_tiles[h], h, 3, 0) for h in range(2)]
    partner = swap(cache)
    codes, one, three, partner, half = barrier((codes, one, three, partner, half))
    low = [shift(one[h][:2], h, 1, 0) for h in range(2)]
    high = [shift(three[h][2:], h, 3, 0) for h in range(2)]
    last = jnp.where(core == 0, partner[0, -BLOCK:], cache[1, -BLOCK:])
    tail = tail_step(jnp.where(me >= seq_count - 2, last, jnp.zeros_like(last)), 0)
    mine = lax.all_gather(half, "kvh", axis=0, tiled=True)
    low, high, tail = barrier((low, high, tail))

    def attend(e, arrays):
        return attend_slots(e, codes, place, arrays, (cache, partner))

    packed = pack(codes, place, [x for h in range(2) for x in (own_tiles[h], one[h], three[h], low[h], high[h])])
    near = [[shift(packed[h][e], h, 0, e) for h in range(2)] for e in (1, 3)]
    tail = tail_step(tail, 1)
    back0 = attend(0, [packed[h][0] for h in range(2)])
    far = [packed[h][2] for h in range(2)]
    near, far, tail, back0 = barrier((near, far, tail, back0))
    far = [shift(far[h], h, 0, 2) for h in range(2)]
    tail = tail_step(tail, 2)
    out1 = attend(1, near[0])
    out3 = attend(3, near[1])
    far, tail, out1, out3 = barrier((far, tail, out1, out3))
    back1 = [shift(out1[h], h, 0, -1) for h in range(2)]
    back3 = [shift(out3[h], h, 0, -3) for h in range(2)]
    tail = tail_step(tail, 3)
    out2 = attend(2, far)
    back1, back3, tail, out2 = barrier((back1, back3, tail, out2))
    back2 = [shift(out2[h], h, 0, -2) for h in range(2)]
    other = swap(tail)
    tail = jnp.where(core == 0, tail, other), jnp.where(core == 0, other, tail)
    own, lse = attend_local(span_start, queries, span_kv, tail, cache_len)
    back1, back3, back2, own, lse = barrier((back1, back3, back2, own, lse))

    rings = [merge_ring(h, codes, place, (back0[h], back1[h], back2[h], back3[h])) for h in range(2)]
    parts = [[rings[h][0]] + [shift(rings[h][d], h, -d, 0) for d in (1, 3, 2)] for h in range(2)]
    parts, mine = barrier((parts, mine))
    other = swap(mine)
    lane = lax.axis_index("kvh").reshape(1)
    attended = merge(lane, own, lse, parts)
    rows = []
    for d in (1, 2, 3):
        rows.append(lax.ppermute(attended[d], "kvh", [(k, (k + d) % 4) for k in range(4)]))
    total = own_projection(attended[0], out_weight)
    mine, other = mine.reshape(4, 512, -1), other.reshape(4, 512, -1)
    return projection(lane, core.reshape(1), total, rows, mine, other)


def solution(mesh):
    in_specs = (
        P("seq", "kvh"),
        P(None, "seq", "kvh"),
        P(None, "seq", "kvh"),
        P("kvh", "seq", None),
        P("kvh", "seq", None),
        P(),
        P("kvh", None),
    )
    out_specs = P(("seq", "kvh"), None)
    return jax.shard_map(shards, mesh=mesh, in_specs=in_specs, out_specs=out_specs, check_vma=False)
```

```python
import functools
import math

import jax
import jax.numpy as jnp
from jax import lax
from jax.experimental import pallas as pl
from jax.experimental.pallas import tpu as pltpu
from jax.sharding import PartitionSpec as P

TILE = 128
BLOCK = 512
HD = 128
GROUP = 4
ROWS = GROUP * TILE
PAYLOAD = ROWS + 16
VMEM_LIMIT = 16 * 1024 * 1024
COEF = math.log2(math.e) / math.sqrt(HD)


SMALL = pl.CostEstimate(flops=1 << 20, bytes_accessed=1 << 16, transcendentals=0)


def params():
    return pltpu.CompilerParams(vmem_limit_bytes=VMEM_LIMIT)


def pinned(*arrays):
    return [pltpu.with_memory_space_constraint(x, pltpu.HBM) for x in arrays]


def position(me):
    return me >> 3, (me >> 1) & 3, me & 1


def device(z, y, c):
    return ((z & 3) << 3) | ((y & 3) << 1) | c


def moved(h, place, first, second, flip):
    z, y, c = place
    if h == 0:
        return device(z + second, y + first, c ^ flip)
    return device(z + first, y + second, c ^ flip)


def code_at(codes, h, asker, owner):
    return codes[(asker * 2 + h) * 32 + owner]


def eye_mask():
    a = lax.broadcasted_iota(jnp.int32, (TILE, TILE), 0)
    b = lax.broadcasted_iota(jnp.int32, (TILE, TILE), 1)
    return a == b


def softmax_part(q, k, values_ones, allowed=None):
    s = lax.dot_general(q, k, (((1,), (1,)), ((), ())), preferred_element_type=jnp.float32)
    if allowed is not None:
        s = jnp.where(allowed, s, jnp.float32(-1e30))
    m = jnp.max(s, axis=1, keepdims=True)
    p = jnp.exp2((s - m) * COEF).astype(jnp.bfloat16)
    both = jnp.dot(p, values_ones, preferred_element_type=jnp.float32)
    total = both[:, HD:]
    return both[:, :HD] / total, m * COEF + jnp.log2(total)


def with_ones(v):
    return jnp.concatenate([v, jnp.ones_like(v)], axis=1)


def to_row(column, eye):
    return jnp.sum(jnp.where(eye, column, 0.0), axis=0, keepdims=True)


def to_column(row, eye):
    return jnp.sum(jnp.where(eye, row, 0.0), axis=1, keepdims=True)


def split_kernel(q_ref, out0, out1):
    for h, out in enumerate((out0, out1)):
        for g in range(GROUP):
            out[0, pl.ds(g * TILE, TILE), :] = q_ref[:, (h * GROUP + g) * HD : (h * GROUP + g + 1) * HD]


def split(queries):
    shape = pltpu.HBM((4, ROWS, HD), jnp.bfloat16)
    return pl.pallas_call(
        split_kernel,
        grid=(4,),
        in_specs=[pl.BlockSpec((TILE, queries.shape[1]), lambda t: (t, 0))],
        out_specs=[pl.BlockSpec((1, ROWS, HD), lambda t: (t, 0, 0))] * 2,
        out_shape=[shape, shape],
        compiler_params=params(),
        cost_estimate=SMALL,
        name="split",
    )(*pinned(queries))


def pack_kernel(codes, me, *refs):
    held, outs, sem = refs[:10], refs[10:18], refs[18]
    place = position(me[0])

    def each(act):
        for h in range(2):
            own, one, three, low, high = held[h * 5 : h * 5 + 5]
            for e in range(4):
                for d in range(4):
                    asker = moved(h, place, -d, 0, 0)
                    for f in range(2):
                        code = code_at(codes, h, asker, moved(h, place, 0, e, f))
                        tile = jnp.maximum(code, 0) >> 4
                        n = ((h * 4 + e) * 4 + d) * 2 + f
                        target = outs[h * 4 + e].at[f, d]
                        if d != 2:
                            source = (own, one, None, three)[d]

                            @pl.when(code >= 0)
                            def _():
                                act(pltpu.make_async_copy(source.at[tile], target, sem.at[n]))

                        else:

                            @pl.when((code >= 0) & (tile < 2))
                            def _():
                                act(pltpu.make_async_copy(low.at[tile & 1], target, sem.at[n]))

                            @pl.when((code >= 0) & (tile >= 2))
                            def _():
                                act(pltpu.make_async_copy(high.at[tile & 1], target, sem.at[n]))

    each(lambda copy: copy.start())
    each(lambda copy: copy.wait())


def pack(codes, me, held):
    shape = pltpu.HBM((2, 4, ROWS, HD), jnp.bfloat16)

    def whole(x):
        return pl.BlockSpec(x.shape, lambda i, c, m: (0, 0, 0))

    outs = pl.pallas_call(
        pack_kernel,
        grid_spec=pltpu.PrefetchScalarGridSpec(
            num_scalar_prefetch=2,
            grid=(1,),
            in_specs=[whole(x) for x in held],
            out_specs=[pl.BlockSpec(memory_space=pltpu.HBM)] * 8,
            scratch_shapes=[pltpu.SemaphoreType.DMA((64,))],
        ),
        out_shape=[shape] * 8,
        compiler_params=params(),
        cost_estimate=SMALL,
        name="pack",
    )(codes, me, *pinned(*held))
    return outs[:4], outs[4:]


def half_kernel(core, w_ref, o_ref):
    o_ref[...] = w_ref[...]


def half_rows(core, weights):
    rows, columns = weights.shape[0] // 8, weights.shape[1]
    return pl.pallas_call(
        half_kernel,
        grid_spec=pltpu.PrefetchScalarGridSpec(
            num_scalar_prefetch=1,
            grid=(4,),
            in_specs=[pl.BlockSpec((rows, columns), lambda i, c: (c[0] * 4 + i, 0))],
            out_specs=pl.BlockSpec((rows, columns), lambda i, c: (i, 0)),
        ),
        out_shape=pltpu.HBM((rows * 4, columns), weights.dtype),
        compiler_params=params(),
        cost_estimate=SMALL,
        name="half",
    )(core, *pinned(weights))


ITEMS = [(h, f) for h in range(2) for f in range(2)]


def lse_parts(lse):
    first = lse.astype(jnp.bfloat16).astype(jnp.float32)
    rest = lse - first
    second = rest.astype(jnp.bfloat16).astype(jnp.float32)
    third = rest - second
    parts = jnp.concatenate([first, second, third, jnp.zeros_like(third)], axis=0)
    return parts.astype(jnp.bfloat16)


def lse_rows(parts):
    parts = parts.astype(jnp.float32)
    return parts[0:4] + parts[4:8] + parts[8:12]


def slot_code(e, item, d, codes, me):
    h, f = item
    asker = moved(h, position(me[0]), -d, -e, 0)
    return code_at(codes, h, asker, me[0] ^ f)


def slot_kernel(*refs):
    n = len(ITEMS)
    refs = refs[2:]
    qs, ks, vs, outs = refs[:2], refs[2 : 2 + n], refs[2 + n : 2 + 2 * n], refs[2 + 2 * n :]
    eye = eye_mask()
    for i, (h, f) in enumerate(ITEMS):
        k = ks[i][0]
        vo = with_ones(vs[i][0])
        rows = []
        for g in range(GROUP):
            at = pl.ds(g * TILE, TILE)
            o, lse = softmax_part(qs[h][f, 0, at, :], k, vo)
            outs[h][f, 0, at, :] = o.astype(jnp.bfloat16)
            rows.append(to_row(lse, eye))
        outs[h][f, 0, pl.ds(ROWS, 16), :] = lse_parts(jnp.concatenate(rows, axis=0))


def attend_slots(e, codes, me, arrays, caches):
    n = len(ITEMS)

    def block(which, item):
        def index(d, codes, me):
            return which, jnp.maximum(slot_code(e, item, d, codes, me), 0) & 15, item[0]

        return pl.BlockSpec((1, BLOCK, HD), index)

    return pl.pallas_call(
        slot_kernel,
        grid_spec=pltpu.PrefetchScalarGridSpec(
            num_scalar_prefetch=2,
            grid=(4,),
            in_specs=[pl.BlockSpec((2, 1, ROWS, HD), lambda d, c, m: (0, d, 0, 0))] * 2
            + [block(0, item) for item in ITEMS]
            + [block(1, item) for item in ITEMS],
            out_specs=[pl.BlockSpec((2, 1, PAYLOAD, HD), lambda d, c, m: (0, d, 0, 0))] * 2,
        ),
        out_shape=[pltpu.HBM((2, 4, PAYLOAD, HD), jnp.bfloat16)] * 2,
        compiler_params=params(),
        cost_estimate=SMALL,
        name="slots",
    )(codes, me, *pinned(*arrays), *pinned(*([caches[f] for _, f in ITEMS] * 2)))


def local_kernel(start, q_ref, own_ref, tailk_ref, tailv_ref, o_ref, lse_ref, *, tail_base):
    t = pl.program_id(1)
    eye = eye_mask()
    k = jnp.concatenate([own_ref[0], tailk_ref[...]], axis=0)
    vo = with_ones(jnp.concatenate([own_ref[1], tailv_ref[...]], axis=0))
    key = lax.broadcasted_iota(jnp.int32, (TILE, 2 * BLOCK), 1)
    row = lax.broadcasted_iota(jnp.int32, (TILE, 2 * BLOCK), 0)
    limit = jnp.where(key < BLOCK, t * TILE + row + 1, start[0] - tail_base + 2 * BLOCK)
    allowed = key < limit
    for g in range(GROUP):
        o, lse = softmax_part(q_ref[:, g * HD : (g + 1) * HD], k, vo, allowed)
        o_ref[0, 0, g] = o
        lse_ref[0, 0, pl.ds(g, 1), :] = to_row(lse, eye)


def attend_local(start, queries, span_kv, tail, tail_base):
    one = pl.BlockSpec((BLOCK, HD), lambda h, t, s: (0, h))
    kv = pl.BlockSpec((2, BLOCK, HD), lambda h, t, s: (0, 0, h))
    return pl.pallas_call(
        functools.partial(local_kernel, tail_base=tail_base),
        grid_spec=pltpu.PrefetchScalarGridSpec(
            num_scalar_prefetch=1,
            grid=(2, 4),
            in_specs=[pl.BlockSpec((TILE, GROUP * HD), lambda h, t, s: (t, h)), kv, one, one],
            out_specs=[
                pl.BlockSpec((1, 1, GROUP, TILE, HD), lambda h, t, s: (h, t, 0, 0, 0)),
                pl.BlockSpec((1, 1, 8, TILE), lambda h, t, s: (h, t, 0, 0)),
            ],
        ),
        out_shape=[
            pltpu.HBM((2, 4, GROUP, TILE, HD), jnp.float32),
            pltpu.HBM((2, 4, 8, TILE), jnp.float32),
        ],
        compiler_params=params(),
        cost_estimate=SMALL,
        name="local",
    )(start, *pinned(queries, span_kv, *tail))


def ring_kernel(h, codes, me, *refs):
    slots, outs = refs[:4], refs[4:8]
    sums, lses, packed, sem = refs[8:]
    d = pl.program_id(0)
    place = position(me[0])
    asker = moved(h, place, -d, 0, 0)
    eye = eye_mask()
    sums[...] = jnp.zeros_like(sums)
    lses[...] = jnp.full(lses.shape, -1e30, jnp.float32)
    for e in range(4):
        for f in range(2):
            code = code_at(codes, h, asker, moved(h, place, 0, e, f))
            ref = slots[e].at[f]

            @pl.when(code >= 0)
            def _():
                t = jnp.maximum(code, 0) >> 4
                old = lses[t, 0:4]
                new = lse_rows(ref[0, pl.ds(ROWS, 16), :])
                top = jnp.maximum(old, new)
                weight_old = jnp.exp2(old - top)
                weight_new = jnp.exp2(new - top)
                total = weight_old + weight_new
                lses[t, 0:4] = top + jnp.log2(total)
                share = weight_new / total
                for g in range(GROUP):
                    at = pl.ds(g * TILE, TILE)
                    before = sums[t, at, :]
                    change = ref[0, at, :].astype(jnp.float32) - before
                    sums[t, at, :] = before + to_column(share[g : g + 1], eye) * change

    for t in range(4):
        packed[d & 1, t, pl.ds(0, ROWS), :] = sums[t].astype(jnp.bfloat16)
        packed[d & 1, t, pl.ds(ROWS, 16), :] = lse_parts(lses[t, 0:4])
    copies = [pltpu.make_async_copy(packed.at[n % 2], outs[n], sem.at[n % 2]) for n in range(4)]
    for n in range(4):

        @pl.when(d == n)
        def _():
            copies[n].start()
            if n > 0:
                copies[n - 1].wait()
            if n == 3:
                copies[n].wait()


def merge_ring(h, codes, me, slots):
    return pl.pallas_call(
        functools.partial(ring_kernel, h),
        grid_spec=pltpu.PrefetchScalarGridSpec(
            num_scalar_prefetch=2,
            grid=(4,),
            in_specs=[pl.BlockSpec((2, 1, PAYLOAD, HD), lambda d, c, m: (0, d, 0, 0))] * 4,
            out_specs=[pl.BlockSpec(memory_space=pltpu.HBM)] * 4,
            scratch_shapes=[
                pltpu.VMEM((4, ROWS, HD), jnp.float32),
                pltpu.VMEM((4, 8, HD), jnp.float32),
                pltpu.VMEM((2, 4, PAYLOAD, HD), jnp.bfloat16),
                pltpu.SemaphoreType.DMA((2,)),
            ],
        ),
        out_shape=[pltpu.HBM((4, PAYLOAD, HD), jnp.bfloat16)] * 4,
        compiler_params=params(),
        cost_estimate=SMALL,
        name="ring",
    )(codes, me, *pinned(*slots))


def merge_kernel(own_ref, lse_ref, *refs):
    parts, o_ref = refs[:8], refs[8]
    eye = eye_mask()
    for h in range(2):
        arrived = parts[4 * h : 4 * h + 4]
        rows = [lse_ref[h, 0, 0:4, :]] + [lse_rows(ref[0, pl.ds(ROWS, 16), :]) for ref in arrived]
        top = functools.reduce(jnp.maximum, rows)
        weights = [jnp.exp2(x - top) for x in rows]
        total = functools.reduce(jnp.add, weights)
        weights = [w / total for w in weights]
        for g in range(GROUP):
            sums = [own_ref[h, 0, g]] + [ref[0, pl.ds(g * TILE, TILE), :].astype(jnp.float32) for ref in arrived]
            terms = [to_column(w[g : g + 1], eye) * (x - sums[0]) for w, x in zip(weights[1:], sums[1:])]
            at = (h * GROUP + g) * HD
            o_ref[0, :, at : at + HD] = functools.reduce(jnp.add, terms, sums[0]).astype(jnp.bfloat16)


def merge(lane, own, lse, parts):
    part = pl.BlockSpec((1, PAYLOAD, HD), lambda d, k: ((k[0] + d) & 3, 0, 0))
    return pl.pallas_call(
        lambda lane, *refs: merge_kernel(*refs),
        grid_spec=pltpu.PrefetchScalarGridSpec(
            num_scalar_prefetch=1,
            grid=(4,),
            in_specs=[
                pl.BlockSpec((2, 1, GROUP, TILE, HD), lambda d, k: (0, (k[0] + d) & 3, 0, 0, 0)),
                pl.BlockSpec((2, 1, 8, TILE), lambda d, k: (0, (k[0] + d) & 3, 0, 0)),
            ]
            + [part] * 8,
            out_specs=pl.BlockSpec((1, TILE, 2 * GROUP * HD), lambda d, k: (d, 0, 0)),
        ),
        out_shape=jax.ShapeDtypeStruct((4, TILE, 2 * GROUP * HD), jnp.bfloat16),
        compiler_params=params(),
        cost_estimate=SMALL,
        name="merge",
    )(lane, *pinned(own, lse, *parts[0], *parts[1]))


def own_projection_kernel(x_ref, w_ref, o_ref):
    o_ref[...] = jnp.dot(x_ref[...], w_ref[...], preferred_element_type=jnp.float32)


def own_projection(x, weights):
    columns = 1024
    return pl.pallas_call(
        own_projection_kernel,
        grid=(weights.shape[1] // columns,),
        in_specs=[
            pl.BlockSpec(x.shape, lambda j: (0, 0)),
            pl.BlockSpec((weights.shape[0], columns), lambda j: (0, j)),
        ],
        out_specs=pl.BlockSpec((TILE, columns), lambda j: (0, j)),
        out_shape=pltpu.HBM((TILE, weights.shape[1]), jnp.float32),
        compiler_params=params(),
        cost_estimate=SMALL,
        name="own_projection",
    )(x, weights)


def projection_kernel(lane, core, sum_ref, *refs):
    rows, mine, other, o_ref = refs[:3], refs[3:6], refs[6:9], refs[9]
    total = sum_ref[...]
    half = rows[0].shape[1] // 2
    at = pl.multiple_of(core[0] * half, half)
    away = pl.multiple_of((1 - core[0]) * half, half)
    for d in range(3):
        total += jnp.dot(rows[d][:, pl.ds(at, half)], mine[d][0], preferred_element_type=jnp.float32)
        total += jnp.dot(rows[d][:, pl.ds(away, half)], other[d][0], preferred_element_type=jnp.float32)
    o_ref[...] = total


def projection(lane, core, total, rows, mine, other):
    columns = 1024
    width = total.shape[1]

    def weight(d):
        return pl.BlockSpec((1, mine.shape[1], columns), lambda j, k, c: ((k[0] - d) & 3, 0, j))

    block = pl.BlockSpec((TILE, columns), lambda j, k, c: (0, j))
    return pl.pallas_call(
        projection_kernel,
        grid_spec=pltpu.PrefetchScalarGridSpec(
            num_scalar_prefetch=2,
            grid=(width // columns,),
            in_specs=[block]
            + [pl.BlockSpec(x.shape, lambda j, k, c: (0, 0)) for x in rows]
            + [weight(d) for d in (1, 2, 3)] * 2,
            out_specs=block,
        ),
        out_shape=jax.ShapeDtypeStruct(total.shape, jnp.float32),
        compiler_params=pltpu.CompilerParams(vmem_limit_bytes=2 * VMEM_LIMIT),
        cost_estimate=SMALL,
        name="projection",
    )(lane, core, *pinned(total, *rows), *([mine] * 3), *([other] * 3))


def shift(x, h, first, second, flip=0):
    pairs = [(i, moved(h, position(i), first, second, flip)) for i in range(32)]
    return lax.ppermute(x, "seq", pairs)


def tail_step(tail, step):
    if step == 0:
        pairs = [(device(3, 3, c), device(3, 0, c)) for c in range(2)]
    elif step == 1:
        pairs = [(device(3, a, c), device(3, b, c)) for a, b in ((3, 2), (0, 1)) for c in range(2)]
    elif step == 2:
        pairs = [(device(3, y, c), device(0, y, c)) for y in range(4) for c in range(2)]
    else:
        pairs = [(device(a, y, c), device(b, y, c)) for a, b in ((3, 2), (0, 1)) for y in range(4) for c in range(2)]
    return tail + lax.ppermute(tail, "seq", pairs)


def swap(x):
    return shift(x, 0, 0, 0, 1)


def all_to_all(x, axis):
    return lax.all_to_all(x, axis, split_axis=0, concat_axis=0, tiled=True)


def shards(queries, span_kv, cache, block_group, block_within, span_start, out_weight):
    seq_count = lax.axis_size("seq")
    me = lax.axis_index("seq")
    core = me & 1
    cache_len = cache.shape[1] * seq_count

    hits = block_group[:, None] == jnp.arange(seq_count, dtype=jnp.int32)[None, :, None, None]
    tiles = jnp.arange(4, dtype=jnp.int32)[None, None, :, None]
    code = jnp.sum(jnp.where(hits, block_within[:, None] + tiles * 16 + 1, 0), axis=(2, 3)) - 1
    codes = all_to_all(jnp.broadcast_to(code.reshape(1, -1), (seq_count, 2 * seq_count)), "seq").reshape(-1)
    place = me.reshape(1)

    barrier = lax.optimization_barrier
    own_tiles = split(queries)
    own_tiles, weights = barrier((own_tiles, out_weight))
    half = half_rows(core.reshape(1), weights)
    one = [shift(own_tiles[h], h, 1, 0) for h in range(2)]
    three = [shift(own_tiles[h], h, 3, 0) for h in range(2)]
    partner = swap(cache)
    codes, one, three, partner, half = barrier((codes, one, three, partner, half))
    low = [shift(one[h][:2], h, 1, 0) for h in range(2)]
    high = [shift(three[h][2:], h, 3, 0) for h in range(2)]
    last = jnp.where(core == 0, partner[0, -BLOCK:], cache[1, -BLOCK:])
    tail = tail_step(jnp.where(me >= seq_count - 2, last, jnp.zeros_like(last)), 0)
    mine = lax.all_gather(half, "kvh", axis=0, tiled=True)
    low, high, tail = barrier((low, high, tail))

    def attend(e, arrays):
        return attend_slots(e, codes, place, arrays, (cache, partner))

    packed = pack(codes, place, [x for h in range(2) for x in (own_tiles[h], one[h], three[h], low[h], high[h])])
    near = [[shift(packed[h][e], h, 0, e) for h in range(2)] for e in (1, 3)]
    tail = tail_step(tail, 1)
    back0 = attend(0, [packed[h][0] for h in range(2)])
    far = [packed[h][2] for h in range(2)]
    near, far, tail, back0 = barrier((near, far, tail, back0))
    far = [shift(far[h], h, 0, 2) for h in range(2)]
    tail = tail_step(tail, 2)
    out1 = attend(1, near[0])
    out3 = attend(3, near[1])
    far, tail, out1, out3 = barrier((far, tail, out1, out3))
    back1 = [shift(out1[h], h, 0, -1) for h in range(2)]
    back3 = [shift(out3[h], h, 0, -3) for h in range(2)]
    tail = tail_step(tail, 3)
    out2 = attend(2, far)
    back1, back3, tail, out2 = barrier((back1, back3, tail, out2))
    back2 = [shift(out2[h], h, 0, -2) for h in range(2)]
    other = swap(tail)
    tail = jnp.where(core == 0, tail, other), jnp.where(core == 0, other, tail)
    own, lse = attend_local(span_start, queries, span_kv, tail, cache_len)
    back1, back3, back2, own, lse = barrier((back1, back3, back2, own, lse))

    rings = [merge_ring(h, codes, place, (back0[h], back1[h], back2[h], back3[h])) for h in range(2)]
    parts = [[rings[h][0]] + [shift(rings[h][d], h, -d, 0) for d in (1, 3, 2)] for h in range(2)]
    parts, mine = barrier((parts, mine))
    other = swap(mine)
    lane = lax.axis_index("kvh").reshape(1)
    attended = merge(lane, own, lse, parts)
    rows = []
    for d in (1, 2, 3):
        rows.append(lax.ppermute(attended[d], "kvh", [(k, (k + d) % 4) for k in range(4)]))
    total = own_projection(attended[0], out_weight)
    mine, other = mine.reshape(4, 512, -1), other.reshape(4, 512, -1)
    return projection(lane, core.reshape(1), total, rows, mine, other)


def solution(mesh):
    in_specs = (
        P("seq", "kvh"),
        P(None, "seq", "kvh"),
        P(None, "seq", "kvh"),
        P("kvh", "seq", None),
        P("kvh", "seq", None),
        P(),
        P("kvh", None),
    )
    out_specs = P(("seq", "kvh"), None)
    return jax.shard_map(shards, mesh=mesh, in_specs=in_specs, out_specs=out_specs, check_vma=False)
```

```python
import functools
import math

import jax
import jax.numpy as jnp
from jax import lax
from jax.experimental import pallas as pl
from jax.experimental.pallas import tpu as pltpu
from jax.sharding import PartitionSpec as P

TILE = 128
BLOCK = 512
HD = 128
GROUP = 4
ROWS = GROUP * TILE
PAYLOAD = ROWS + 16
VMEM_LIMIT = 16 * 1024 * 1024
COEF = math.log2(math.e) / math.sqrt(HD)


SMALL = pl.CostEstimate(flops=1 << 20, bytes_accessed=1 << 16, transcendentals=0)


def params():
    return pltpu.CompilerParams(vmem_limit_bytes=VMEM_LIMIT)


def pinned(*arrays):
    return [pltpu.with_memory_space_constraint(x, pltpu.HBM) for x in arrays]


def position(me):
    return me >> 3, (me >> 1) & 3, me & 1


def device(z, y, c):
    return ((z & 3) << 3) | ((y & 3) << 1) | c


def moved(h, place, first, second, flip):
    z, y, c = place
    if h == 0:
        return device(z + second, y + first, c ^ flip)
    return device(z + first, y + second, c ^ flip)


def code_at(codes, h, asker, owner):
    return codes[(asker * 2 + h) * 32 + owner]


def eye_mask():
    a = lax.broadcasted_iota(jnp.int32, (TILE, TILE), 0)
    b = lax.broadcasted_iota(jnp.int32, (TILE, TILE), 1)
    return a == b


def softmax_part(q, k, values_ones, allowed=None):
    s = lax.dot_general(q, k, (((1,), (1,)), ((), ())), preferred_element_type=jnp.float32)
    if allowed is not None:
        s = jnp.where(allowed, s, jnp.float32(-1e30))
    m = jnp.max(s, axis=1, keepdims=True)
    p = jnp.exp2((s - m) * COEF).astype(jnp.bfloat16)
    both = jnp.dot(p, values_ones, preferred_element_type=jnp.float32)
    total = both[:, HD:]
    return both[:, :HD] / total, m * COEF + jnp.log2(total)


def with_ones(v):
    return jnp.concatenate([v, jnp.ones_like(v)], axis=1)


def to_row(column, eye):
    return jnp.sum(jnp.where(eye, column, 0.0), axis=0, keepdims=True)


def to_column(row, eye):
    return jnp.sum(jnp.where(eye, row, 0.0), axis=1, keepdims=True)


def split_kernel(q_ref, out0, out1):
    for h, out in enumerate((out0, out1)):
        for g in range(GROUP):
            out[0, pl.ds(g * TILE, TILE), :] = q_ref[:, (h * GROUP + g) * HD : (h * GROUP + g + 1) * HD]


def split(queries):
    shape = pltpu.HBM((4, ROWS, HD), jnp.bfloat16)
    return pl.pallas_call(
        split_kernel,
        grid=(4,),
        in_specs=[pl.BlockSpec((TILE, queries.shape[1]), lambda t: (t, 0))],
        out_specs=[pl.BlockSpec((1, ROWS, HD), lambda t: (t, 0, 0))] * 2,
        out_shape=[shape, shape],
        compiler_params=params(),
        cost_estimate=SMALL,
        name="split",
    )(*pinned(queries))


def pack_kernel(codes, me, *refs):
    held, outs, sem = refs[:10], refs[10:18], refs[18]
    place = position(me[0])

    def each(act):
        for h in range(2):
            own, one, three, low, high = held[h * 5 : h * 5 + 5]
            for e in range(4):
                for d in range(4):
                    asker = moved(h, place, -d, 0, 0)
                    for f in range(2):
                        code = code_at(codes, h, asker, moved(h, place, 0, e, f))
                        tile = jnp.maximum(code, 0) >> 4
                        n = ((h * 4 + e) * 4 + d) * 2 + f
                        target = outs[h * 4 + e].at[f, d]
                        if d != 2:
                            source = (own, one, None, three)[d]

                            @pl.when(code >= 0)
                            def _():
                                act(pltpu.make_async_copy(source.at[tile], target, sem.at[n]))

                        else:

                            @pl.when((code >= 0) & (tile < 2))
                            def _():
                                act(pltpu.make_async_copy(low.at[tile & 1], target, sem.at[n]))

                            @pl.when((code >= 0) & (tile >= 2))
                            def _():
                                act(pltpu.make_async_copy(high.at[tile & 1], target, sem.at[n]))

    each(lambda copy: copy.start())
    each(lambda copy: copy.wait())


def pack(codes, me, held):
    shape = pltpu.HBM((2, 4, ROWS, HD), jnp.bfloat16)

    def whole(x):
        return pl.BlockSpec(x.shape, lambda i, c, m: (0, 0, 0))

    outs = pl.pallas_call(
        pack_kernel,
        grid_spec=pltpu.PrefetchScalarGridSpec(
            num_scalar_prefetch=2,
            grid=(1,),
            in_specs=[whole(x) for x in held],
            out_specs=[pl.BlockSpec(memory_space=pltpu.HBM)] * 8,
            scratch_shapes=[pltpu.SemaphoreType.DMA((64,))],
        ),
        out_shape=[shape] * 8,
        compiler_params=params(),
        cost_estimate=SMALL,
        name="pack",
    )(codes, me, *pinned(*held))
    return outs[:4], outs[4:]


def half_kernel(core, w_ref, o_ref):
    o_ref[...] = w_ref[...]


def half_rows(core, weights):
    rows, columns = weights.shape[0] // 8, weights.shape[1]
    return pl.pallas_call(
        half_kernel,
        grid_spec=pltpu.PrefetchScalarGridSpec(
            num_scalar_prefetch=1,
            grid=(4,),
            in_specs=[pl.BlockSpec((rows, columns), lambda i, c: (c[0] * 4 + i, 0))],
            out_specs=pl.BlockSpec((rows, columns), lambda i, c: (i, 0)),
        ),
        out_shape=pltpu.HBM((rows * 4, columns), weights.dtype),
        compiler_params=params(),
        cost_estimate=SMALL,
        name="half",
    )(core, *pinned(weights))


ITEMS = [(h, f) for h in range(2) for f in range(2)]


def lse_parts(lse):
    first = lse.astype(jnp.bfloat16).astype(jnp.float32)
    rest = lse - first
    second = rest.astype(jnp.bfloat16).astype(jnp.float32)
    third = rest - second
    parts = jnp.concatenate([first, second, third, jnp.zeros_like(third)], axis=0)
    return parts.astype(jnp.bfloat16)


def lse_rows(parts):
    parts = parts.astype(jnp.float32)
    return parts[0:4] + parts[4:8] + parts[8:12]


def slot_code(e, item, d, codes, me):
    h, f = item
    asker = moved(h, position(me[0]), -d, -e, 0)
    return code_at(codes, h, asker, me[0] ^ f)


def slot_kernel(*refs):
    n = len(ITEMS)
    refs = refs[2:]
    qs, ks, vs, outs = refs[:2], refs[2 : 2 + n], refs[2 + n : 2 + 2 * n], refs[2 + 2 * n :]
    eye = eye_mask()
    for i, (h, f) in enumerate(ITEMS):
        k = ks[i][0]
        vo = with_ones(vs[i][0])
        rows = []
        for g in range(GROUP):
            at = pl.ds(g * TILE, TILE)
            o, lse = softmax_part(qs[h][f, 0, at, :], k, vo)
            outs[h][f, 0, at, :] = o.astype(jnp.bfloat16)
            rows.append(to_row(lse, eye))
        outs[h][f, 0, pl.ds(ROWS, 16), :] = lse_parts(jnp.concatenate(rows, axis=0))


def attend_slots(e, codes, me, arrays, caches):
    n = len(ITEMS)

    def block(which, item):
        def index(d, codes, me):
            return which, jnp.maximum(slot_code(e, item, d, codes, me), 0) & 15, item[0]

        return pl.BlockSpec((1, BLOCK, HD), index)

    return pl.pallas_call(
        slot_kernel,
        grid_spec=pltpu.PrefetchScalarGridSpec(
            num_scalar_prefetch=2,
            grid=(4,),
            in_specs=[pl.BlockSpec((2, 1, ROWS, HD), lambda d, c, m: (0, d, 0, 0))] * 2
            + [block(0, item) for item in ITEMS]
            + [block(1, item) for item in ITEMS],
            out_specs=[pl.BlockSpec((2, 1, PAYLOAD, HD), lambda d, c, m: (0, d, 0, 0))] * 2,
        ),
        out_shape=[pltpu.HBM((2, 4, PAYLOAD, HD), jnp.bfloat16)] * 2,
        compiler_params=params(),
        cost_estimate=SMALL,
        name="slots",
    )(codes, me, *pinned(*arrays), *pinned(*([caches[f] for _, f in ITEMS] * 2)))


def local_kernel(start, q_ref, own_ref, tailk_ref, tailv_ref, o_ref, lse_ref, *, tail_base):
    t = pl.program_id(1)
    eye = eye_mask()
    k = jnp.concatenate([own_ref[0], tailk_ref[...]], axis=0)
    vo = with_ones(jnp.concatenate([own_ref[1], tailv_ref[...]], axis=0))
    key = lax.broadcasted_iota(jnp.int32, (TILE, 2 * BLOCK), 1)
    row = lax.broadcasted_iota(jnp.int32, (TILE, 2 * BLOCK), 0)
    limit = jnp.where(key < BLOCK, t * TILE + row + 1, start[0] - tail_base + 2 * BLOCK)
    allowed = key < limit
    for g in range(GROUP):
        o, lse = softmax_part(q_ref[:, g * HD : (g + 1) * HD], k, vo, allowed)
        o_ref[0, 0, g] = o
        lse_ref[0, 0, pl.ds(g, 1), :] = to_row(lse, eye)


def attend_local(start, queries, span_kv, tail, tail_base):
    one = pl.BlockSpec((BLOCK, HD), lambda h, t, s: (0, h))
    kv = pl.BlockSpec((2, BLOCK, HD), lambda h, t, s: (0, 0, h))
    return pl.pallas_call(
        functools.partial(local_kernel, tail_base=tail_base),
        grid_spec=pltpu.PrefetchScalarGridSpec(
            num_scalar_prefetch=1,
            grid=(2, 4),
            in_specs=[pl.BlockSpec((TILE, GROUP * HD), lambda h, t, s: (t, h)), kv, one, one],
            out_specs=[
                pl.BlockSpec((1, 1, GROUP, TILE, HD), lambda h, t, s: (h, t, 0, 0, 0)),
                pl.BlockSpec((1, 1, 8, TILE), lambda h, t, s: (h, t, 0, 0)),
            ],
        ),
        out_shape=[
            pltpu.HBM((2, 4, GROUP, TILE, HD), jnp.float32),
            pltpu.HBM((2, 4, 8, TILE), jnp.float32),
        ],
        compiler_params=params(),
        cost_estimate=SMALL,
        name="local",
    )(start, *pinned(queries, span_kv, *tail))


def ring_kernel(h, codes, me, *refs):
    slots, outs = refs[:4], refs[4:8]
    sums, lses, packed, sem = refs[8:]
    d = pl.program_id(0)
    place = position(me[0])
    asker = moved(h, place, -d, 0, 0)
    eye = eye_mask()
    sums[...] = jnp.zeros_like(sums)
    lses[...] = jnp.full(lses.shape, -1e30, jnp.float32)
    for e in range(4):
        for f in range(2):
            code = code_at(codes, h, asker, moved(h, place, 0, e, f))
            ref = slots[e].at[f]

            @pl.when(code >= 0)
            def _():
                t = jnp.maximum(code, 0) >> 4
                old = lses[t, 0:4]
                new = lse_rows(ref[0, pl.ds(ROWS, 16), :])
                top = jnp.maximum(old, new)
                weight_old = jnp.exp2(old - top)
                weight_new = jnp.exp2(new - top)
                total = weight_old + weight_new
                lses[t, 0:4] = top + jnp.log2(total)
                share = weight_new / total
                for g in range(GROUP):
                    at = pl.ds(g * TILE, TILE)
                    before = sums[t, at, :]
                    change = ref[0, at, :].astype(jnp.float32) - before
                    sums[t, at, :] = before + to_column(share[g : g + 1], eye) * change

    for t in range(4):
        packed[d & 1, t, pl.ds(0, ROWS), :] = sums[t].astype(jnp.bfloat16)
        packed[d & 1, t, pl.ds(ROWS, 16), :] = lse_parts(lses[t, 0:4])
    copies = [pltpu.make_async_copy(packed.at[n % 2], outs[n], sem.at[n % 2]) for n in range(4)]
    for n in range(4):

        @pl.when(d == n)
        def _():
            copies[n].start()
            if n > 0:
                copies[n - 1].wait()
            if n == 3:
                copies[n].wait()


def merge_ring(h, codes, me, slots):
    return pl.pallas_call(
        functools.partial(ring_kernel, h),
        grid_spec=pltpu.PrefetchScalarGridSpec(
            num_scalar_prefetch=2,
            grid=(4,),
            in_specs=[pl.BlockSpec((2, 1, PAYLOAD, HD), lambda d, c, m: (0, d, 0, 0))] * 4,
            out_specs=[pl.BlockSpec(memory_space=pltpu.HBM)] * 4,
            scratch_shapes=[
                pltpu.VMEM((4, ROWS, HD), jnp.float32),
                pltpu.VMEM((4, 8, HD), jnp.float32),
                pltpu.VMEM((2, 4, PAYLOAD, HD), jnp.bfloat16),
                pltpu.SemaphoreType.DMA((2,)),
            ],
        ),
        out_shape=[pltpu.HBM((4, PAYLOAD, HD), jnp.bfloat16)] * 4,
        compiler_params=params(),
        cost_estimate=SMALL,
        name="ring",
    )(codes, me, *pinned(*slots))


def merge_kernel(own_ref, lse_ref, *refs):
    parts, o_ref = refs[:8], refs[8]
    eye = eye_mask()
    for h in range(2):
        arrived = parts[4 * h : 4 * h + 4]
        rows = [lse_ref[h, 0, 0:4, :]] + [lse_rows(ref[0, pl.ds(ROWS, 16), :]) for ref in arrived]
        top = functools.reduce(jnp.maximum, rows)
        weights = [jnp.exp2(x - top) for x in rows]
        total = functools.reduce(jnp.add, weights)
        weights = [w / total for w in weights]
        for g in range(GROUP):
            sums = [own_ref[h, 0, g]] + [ref[0, pl.ds(g * TILE, TILE), :].astype(jnp.float32) for ref in arrived]
            terms = [to_column(w[g : g + 1], eye) * (x - sums[0]) for w, x in zip(weights[1:], sums[1:])]
            at = (h * GROUP + g) * HD
            o_ref[0, :, at : at + HD] = functools.reduce(jnp.add, terms, sums[0]).astype(jnp.bfloat16)


def merge(lane, own, lse, parts):
    part = pl.BlockSpec((1, PAYLOAD, HD), lambda d, k: ((k[0] + d) & 3, 0, 0))
    return pl.pallas_call(
        lambda lane, *refs: merge_kernel(*refs),
        grid_spec=pltpu.PrefetchScalarGridSpec(
            num_scalar_prefetch=1,
            grid=(4,),
            in_specs=[
                pl.BlockSpec((2, 1, GROUP, TILE, HD), lambda d, k: (0, (k[0] + d) & 3, 0, 0, 0)),
                pl.BlockSpec((2, 1, 8, TILE), lambda d, k: (0, (k[0] + d) & 3, 0, 0)),
            ]
            + [part] * 8,
            out_specs=pl.BlockSpec((1, TILE, 2 * GROUP * HD), lambda d, k: (d, 0, 0)),
        ),
        out_shape=jax.ShapeDtypeStruct((4, TILE, 2 * GROUP * HD), jnp.bfloat16),
        compiler_params=params(),
        cost_estimate=SMALL,
        name="merge",
    )(lane, *pinned(own, lse, *parts[0], *parts[1]))


def own_projection_kernel(x_ref, w_ref, o_ref):
    o_ref[...] = jnp.dot(x_ref[...], w_ref[...], preferred_element_type=jnp.float32)


def own_projection(x, weights):
    columns = 1024
    return pl.pallas_call(
        own_projection_kernel,
        grid=(weights.shape[1] // columns,),
        in_specs=[
            pl.BlockSpec(x.shape, lambda j: (0, 0)),
            pl.BlockSpec((weights.shape[0], columns), lambda j: (0, j)),
        ],
        out_specs=pl.BlockSpec((TILE, columns), lambda j: (0, j)),
        out_shape=pltpu.HBM((TILE, weights.shape[1]), jnp.float32),
        compiler_params=params(),
        cost_estimate=SMALL,
        name="own_projection",
    )(x, weights)


def projection_kernel(lane, core, sum_ref, *refs):
    rows, mine, other, o_ref = refs[:3], refs[3:6], refs[6:9], refs[9]
    total = sum_ref[...]
    half = rows[0].shape[1] // 2
    at = pl.multiple_of(core[0] * half, half)
    away = pl.multiple_of((1 - core[0]) * half, half)
    for d in range(3):
        total += jnp.dot(rows[d][:, pl.ds(at, half)], mine[d][0], preferred_element_type=jnp.float32)
        total += jnp.dot(rows[d][:, pl.ds(away, half)], other[d][0], preferred_element_type=jnp.float32)
    o_ref[...] = total


def projection(lane, core, total, rows, mine, other):
    columns = 1024
    width = total.shape[1]

    def weight(d):
        return pl.BlockSpec((1, mine.shape[1], columns), lambda j, k, c: ((k[0] - d) & 3, 0, j))

    block = pl.BlockSpec((TILE, columns), lambda j, k, c: (0, j))
    return pl.pallas_call(
        projection_kernel,
        grid_spec=pltpu.PrefetchScalarGridSpec(
            num_scalar_prefetch=2,
            grid=(width // columns,),
            in_specs=[block]
            + [pl.BlockSpec(x.shape, lambda j, k, c: (0, 0)) for x in rows]
            + [weight(d) for d in (1, 2, 3)] * 2,
            out_specs=block,
        ),
        out_shape=jax.ShapeDtypeStruct(total.shape, jnp.float32),
        compiler_params=pltpu.CompilerParams(vmem_limit_bytes=2 * VMEM_LIMIT),
        cost_estimate=SMALL,
        name="projection",
    )(lane, core, *pinned(total, *rows), *([mine] * 3), *([other] * 3))


def shift(x, h, first, second, flip=0):
    pairs = [(i, moved(h, position(i), first, second, flip)) for i in range(32)]
    return lax.ppermute(x, "seq", pairs)


def tail_step(tail, step):
    if step == 0:
        pairs = [(device(3, 3, c), device(3, 0, c)) for c in range(2)]
    elif step == 1:
        pairs = [(device(3, a, c), device(3, b, c)) for a, b in ((3, 2), (0, 1)) for c in range(2)]
    elif step == 2:
        pairs = [(device(3, y, c), device(0, y, c)) for y in range(4) for c in range(2)]
    else:
        pairs = [(device(a, y, c), device(b, y, c)) for a, b in ((3, 2), (0, 1)) for y in range(4) for c in range(2)]
    return tail + lax.ppermute(tail, "seq", pairs)


def swap(x):
    return shift(x, 0, 0, 0, 1)


def all_to_all(x, axis):
    return lax.all_to_all(x, axis, split_axis=0, concat_axis=0, tiled=True)


def shards(queries, span_kv, cache, block_group, block_within, span_start, out_weight):
    seq_count = lax.axis_size("seq")
    me = lax.axis_index("seq")
    core = me & 1
    cache_len = cache.shape[1] * seq_count

    hits = block_group[:, None] == jnp.arange(seq_count, dtype=jnp.int32)[None, :, None, None]
    tiles = jnp.arange(4, dtype=jnp.int32)[None, None, :, None]
    code = jnp.sum(jnp.where(hits, block_within[:, None] + tiles * 16 + 1, 0), axis=(2, 3)) - 1
    codes = all_to_all(jnp.broadcast_to(code.reshape(1, -1), (seq_count, 2 * seq_count)), "seq").reshape(-1)
    place = me.reshape(1)

    barrier = lax.optimization_barrier
    own_tiles = split(queries)
    own_tiles, weights = barrier((own_tiles, out_weight))
    half = half_rows(core.reshape(1), weights)
    one = [shift(own_tiles[h], h, 1, 0) for h in range(2)]
    three = [shift(own_tiles[h], h, 3, 0) for h in range(2)]
    last = cache[:, -BLOCK:]
    tail = jnp.where(me == seq_count - 1, last[1], lax.ppermute(last[0], "seq", [(31, 30)]))
    tail = tail_step(tail, 0)
    codes, one, three, tail, half = barrier((codes, one, three, tail, half))
    mine = lax.all_gather(half, "kvh", axis=0, tiled=True)
    low = [shift(one[h][:2], h, 1, 0) for h in range(2)]
    high = [shift(three[h][2:], h, 3, 0) for h in range(2)]
    tail = tail_step(tail, 1)
    partner = swap(cache)
    low, high, tail, partner = barrier((low, high, tail, partner))

    def attend(e, arrays):
        return attend_slots(e, codes, place, arrays, (cache, partner))

    packed = pack(codes, place, [x for h in range(2) for x in (own_tiles[h], one[h], three[h], low[h], high[h])])
    near = [[shift(packed[h][e], h, 0, e) for h in range(2)] for e in (1, 3)]
    tail = tail_step(tail, 2)
    back0 = attend(0, [packed[h][0] for h in range(2)])
    far = [packed[h][2] for h in range(2)]
    near, far, tail, back0 = barrier((near, far, tail, back0))
    far = [shift(far[h], h, 0, 2) for h in range(2)]
    tail = tail_step(tail, 3)
    out1 = attend(1, near[0])
    out3 = attend(3, near[1])
    far, tail, out1, out3 = barrier((far, tail, out1, out3))
    back1 = [shift(out1[h], h, 0, -1) for h in range(2)]
    back3 = [shift(out3[h], h, 0, -3) for h in range(2)]
    out2 = attend(2, far)
    back1, back3, tail, out2 = barrier((back1, back3, tail, out2))
    back2 = [shift(out2[h], h, 0, -2) for h in range(2)]
    other = swap(tail)
    tail = jnp.where(core == 0, tail, other), jnp.where(core == 0, other, tail)
    own, lse = attend_local(span_start, queries, span_kv, tail, cache_len)
    back1, back3, back2, own, lse = barrier((back1, back3, back2, own, lse))

    rings = [merge_ring(h, codes, place, (back0[h], back1[h], back2[h], back3[h])) for h in range(2)]
    parts = [[rings[h][0]] + [shift(rings[h][d], h, -d, 0) for d in (1, 3, 2)] for h in range(2)]
    parts, mine = barrier((parts, mine))
    other = swap(mine)
    lane = lax.axis_index("kvh").reshape(1)
    attended = merge(lane, own, lse, parts)
    rows = []
    for d in (1, 2, 3):
        rows.append(lax.ppermute(attended[d], "kvh", [(k, (k + d) % 4) for k in range(4)]))
    total = own_projection(attended[0], out_weight)
    mine, other = mine.reshape(4, 512, -1), other.reshape(4, 512, -1)
    return projection(lane, core.reshape(1), total, rows, mine, other)


def solution(mesh):
    in_specs = (
        P("seq", "kvh"),
        P(None, "seq", "kvh"),
        P(None, "seq", "kvh"),
        P("kvh", "seq", None),
        P("kvh", "seq", None),
        P(),
        P("kvh", None),
    )
    out_specs = P(("seq", "kvh"), None)
    return jax.shard_map(shards, mesh=mesh, in_specs=in_specs, out_specs=out_specs, check_vma=False)
```

```python
import functools
import math

import jax
import jax.numpy as jnp
from jax import lax
from jax.experimental import pallas as pl
from jax.experimental.pallas import tpu as pltpu
from jax.sharding import PartitionSpec as P

TILE = 128
BLOCK = 512
HD = 128
GROUP = 4
ROWS = GROUP * TILE
PAYLOAD = ROWS + 16
VMEM_LIMIT = 16 * 1024 * 1024
COEF = math.log2(math.e) / math.sqrt(HD)


SMALL = pl.CostEstimate(flops=1 << 20, bytes_accessed=1 << 16, transcendentals=0)


def params():
    return pltpu.CompilerParams(vmem_limit_bytes=VMEM_LIMIT)


def pinned(*arrays):
    return [pltpu.with_memory_space_constraint(x, pltpu.HBM) for x in arrays]


def position(me):
    return me >> 3, (me >> 1) & 3, me & 1


def device(z, y, c):
    return ((z & 3) << 3) | ((y & 3) << 1) | c


def moved(h, place, first, second, flip):
    z, y, c = place
    if h == 0:
        return device(z + second, y + first, c ^ flip)
    return device(z + first, y + second, c ^ flip)


def code_at(codes, h, asker, owner):
    return codes[(asker * 2 + h) * 32 + owner]


def eye_mask():
    a = lax.broadcasted_iota(jnp.int32, (TILE, TILE), 0)
    b = lax.broadcasted_iota(jnp.int32, (TILE, TILE), 1)
    return a == b


def softmax_part(q, k, values_ones, allowed=None):
    s = lax.dot_general(q, k, (((1,), (1,)), ((), ())), preferred_element_type=jnp.float32)
    if allowed is not None:
        s = jnp.where(allowed, s, jnp.float32(-1e30))
    m = jnp.max(s, axis=1, keepdims=True)
    p = jnp.exp2((s - m) * COEF).astype(jnp.bfloat16)
    both = jnp.dot(p, values_ones, preferred_element_type=jnp.float32)
    total = both[:, HD:]
    return both[:, :HD] / total, m * COEF + jnp.log2(total)


def with_ones(v):
    return jnp.concatenate([v, jnp.ones_like(v)], axis=1)


def to_row(column, eye):
    return jnp.sum(jnp.where(eye, column, 0.0), axis=0, keepdims=True)


def to_column(row, eye):
    return jnp.sum(jnp.where(eye, row, 0.0), axis=1, keepdims=True)


def split_kernel(q_ref, out0, out1):
    for h, out in enumerate((out0, out1)):
        for g in range(GROUP):
            out[0, pl.ds(g * TILE, TILE), :] = q_ref[:, (h * GROUP + g) * HD : (h * GROUP + g + 1) * HD]


def split(queries):
    shape = pltpu.HBM((4, ROWS, HD), jnp.bfloat16)
    return pl.pallas_call(
        split_kernel,
        grid=(4,),
        in_specs=[pl.BlockSpec((TILE, queries.shape[1]), lambda t: (t, 0))],
        out_specs=[pl.BlockSpec((1, ROWS, HD), lambda t: (t, 0, 0))] * 2,
        out_shape=[shape, shape],
        compiler_params=params(),
        cost_estimate=SMALL,
        name="split",
    )(*pinned(queries))


def pack_kernel(codes, me, *refs):
    held, outs, sem = refs[:10], refs[10:18], refs[18]
    place = position(me[0])

    def each(act):
        for h in range(2):
            own, one, three, low, high = held[h * 5 : h * 5 + 5]
            for e in range(4):
                for d in range(4):
                    asker = moved(h, place, -d, 0, 0)
                    for f in range(2):
                        code = code_at(codes, h, asker, moved(h, place, 0, e, f))
                        tile = jnp.maximum(code, 0) >> 4
                        n = ((h * 4 + e) * 4 + d) * 2 + f
                        target = outs[h * 4 + e].at[f, d]
                        if d != 2:
                            source = (own, one, None, three)[d]

                            @pl.when(code >= 0)
                            def _():
                                act(pltpu.make_async_copy(source.at[tile], target, sem.at[n]))

                        else:

                            @pl.when((code >= 0) & (tile < 2))
                            def _():
                                act(pltpu.make_async_copy(low.at[tile & 1], target, sem.at[n]))

                            @pl.when((code >= 0) & (tile >= 2))
                            def _():
                                act(pltpu.make_async_copy(high.at[tile & 1], target, sem.at[n]))

    each(lambda copy: copy.start())
    each(lambda copy: copy.wait())


def pack(codes, me, held):
    shape = pltpu.HBM((2, 4, ROWS, HD), jnp.bfloat16)

    def whole(x):
        return pl.BlockSpec(x.shape, lambda i, c, m: (0, 0, 0))

    outs = pl.pallas_call(
        pack_kernel,
        grid_spec=pltpu.PrefetchScalarGridSpec(
            num_scalar_prefetch=2,
            grid=(1,),
            in_specs=[whole(x) for x in held],
            out_specs=[pl.BlockSpec(memory_space=pltpu.HBM)] * 8,
            scratch_shapes=[pltpu.SemaphoreType.DMA((64,))],
        ),
        out_shape=[shape] * 8,
        compiler_params=params(),
        cost_estimate=SMALL,
        name="pack",
    )(codes, me, *pinned(*held))
    return outs[:4], outs[4:]


def half_kernel(core, w_ref, o_ref):
    o_ref[...] = w_ref[...]


def half_rows(core, weights):
    rows, columns = weights.shape[0] // 8, weights.shape[1]
    return pl.pallas_call(
        half_kernel,
        grid_spec=pltpu.PrefetchScalarGridSpec(
            num_scalar_prefetch=1,
            grid=(4,),
            in_specs=[pl.BlockSpec((rows, columns), lambda i, c: (c[0] * 4 + i, 0))],
            out_specs=pl.BlockSpec((rows, columns), lambda i, c: (i, 0)),
        ),
        out_shape=pltpu.HBM((rows * 4, columns), weights.dtype),
        compiler_params=params(),
        cost_estimate=SMALL,
        name="half",
    )(core, *pinned(weights))


ITEMS = [(h, f) for h in range(2) for f in range(2)]


def lse_parts(lse):
    first = lse.astype(jnp.bfloat16).astype(jnp.float32)
    rest = lse - first
    second = rest.astype(jnp.bfloat16).astype(jnp.float32)
    third = rest - second
    parts = jnp.concatenate([first, second, third, jnp.zeros_like(third)], axis=0)
    return parts.astype(jnp.bfloat16)


def lse_rows(parts):
    parts = parts.astype(jnp.float32)
    return parts[0:4] + parts[4:8] + parts[8:12]


def slot_code(e, item, d, codes, me):
    h, f = item
    asker = moved(h, position(me[0]), -d, -e, 0)
    return code_at(codes, h, asker, me[0] ^ f)


def slot_kernel(*refs):
    n = len(ITEMS)
    refs = refs[2:]
    qs, ks, vs, outs = refs[:2], refs[2 : 2 + n], refs[2 + n : 2 + 2 * n], refs[2 + 2 * n :]
    eye = eye_mask()
    for i, (h, f) in enumerate(ITEMS):
        k = ks[i][0]
        vo = with_ones(vs[i][0])
        rows = []
        for g in range(GROUP):
            at = pl.ds(g * TILE, TILE)
            o, lse = softmax_part(qs[h][f, 0, at, :], k, vo)
            outs[h][f, 0, at, :] = o.astype(jnp.bfloat16)
            rows.append(to_row(lse, eye))
        outs[h][f, 0, pl.ds(ROWS, 16), :] = lse_parts(jnp.concatenate(rows, axis=0))


def attend_slots(e, codes, me, arrays, caches):
    n = len(ITEMS)

    def block(which, item):
        def index(d, codes, me):
            return which, jnp.maximum(slot_code(e, item, d, codes, me), 0) & 15, item[0]

        return pl.BlockSpec((1, BLOCK, HD), index)

    return pl.pallas_call(
        slot_kernel,
        grid_spec=pltpu.PrefetchScalarGridSpec(
            num_scalar_prefetch=2,
            grid=(4,),
            in_specs=[pl.BlockSpec((2, 1, ROWS, HD), lambda d, c, m: (0, d, 0, 0))] * 2
            + [block(0, item) for item in ITEMS]
            + [block(1, item) for item in ITEMS],
            out_specs=[pl.BlockSpec((2, 1, PAYLOAD, HD), lambda d, c, m: (0, d, 0, 0))] * 2,
        ),
        out_shape=[pltpu.HBM((2, 4, PAYLOAD, HD), jnp.bfloat16)] * 2,
        compiler_params=params(),
        cost_estimate=SMALL,
        name="slots",
    )(codes, me, *pinned(*arrays), *pinned(*([caches[f] for _, f in ITEMS] * 2)))


def local_kernel(start, q_ref, own_ref, tailk_ref, tailv_ref, o_ref, lse_ref, *, tail_base):
    t = pl.program_id(1)
    eye = eye_mask()
    k = jnp.concatenate([own_ref[0], tailk_ref[...]], axis=0)
    vo = with_ones(jnp.concatenate([own_ref[1], tailv_ref[...]], axis=0))
    key = lax.broadcasted_iota(jnp.int32, (TILE, 2 * BLOCK), 1)
    row = lax.broadcasted_iota(jnp.int32, (TILE, 2 * BLOCK), 0)
    limit = jnp.where(key < BLOCK, t * TILE + row + 1, start[0] - tail_base + 2 * BLOCK)
    allowed = key < limit
    for g in range(GROUP):
        o, lse = softmax_part(q_ref[:, g * HD : (g + 1) * HD], k, vo, allowed)
        o_ref[0, 0, g] = o
        lse_ref[0, 0, pl.ds(g, 1), :] = to_row(lse, eye)


def attend_local(start, queries, span_kv, tail, tail_base):
    one = pl.BlockSpec((BLOCK, HD), lambda h, t, s: (0, h))
    kv = pl.BlockSpec((2, BLOCK, HD), lambda h, t, s: (0, 0, h))
    return pl.pallas_call(
        functools.partial(local_kernel, tail_base=tail_base),
        grid_spec=pltpu.PrefetchScalarGridSpec(
            num_scalar_prefetch=1,
            grid=(2, 4),
            in_specs=[pl.BlockSpec((TILE, GROUP * HD), lambda h, t, s: (t, h)), kv, one, one],
            out_specs=[
                pl.BlockSpec((1, 1, GROUP, TILE, HD), lambda h, t, s: (h, t, 0, 0, 0)),
                pl.BlockSpec((1, 1, 8, TILE), lambda h, t, s: (h, t, 0, 0)),
            ],
        ),
        out_shape=[
            pltpu.HBM((2, 4, GROUP, TILE, HD), jnp.float32),
            pltpu.HBM((2, 4, 8, TILE), jnp.float32),
        ],
        compiler_params=params(),
        cost_estimate=SMALL,
        name="local",
    )(start, *pinned(queries, span_kv, *tail))


def ring_kernel(h, codes, me, *refs):
    slots, outs = refs[:4], refs[4:8]
    sums, lses, packed, sem = refs[8:]
    d = pl.program_id(0)
    place = position(me[0])
    asker = moved(h, place, -d, 0, 0)
    eye = eye_mask()
    sums[...] = jnp.zeros_like(sums)
    lses[...] = jnp.full(lses.shape, -1e30, jnp.float32)
    for e in range(4):
        for f in range(2):
            code = code_at(codes, h, asker, moved(h, place, 0, e, f))
            ref = slots[e].at[f]

            @pl.when(code >= 0)
            def _():
                t = jnp.maximum(code, 0) >> 4
                old = lses[t, 0:4]
                new = lse_rows(ref[0, pl.ds(ROWS, 16), :])
                top = jnp.maximum(old, new)
                weight_old = jnp.exp2(old - top)
                weight_new = jnp.exp2(new - top)
                total = weight_old + weight_new
                lses[t, 0:4] = top + jnp.log2(total)
                share = weight_new / total
                for g in range(GROUP):
                    at = pl.ds(g * TILE, TILE)
                    before = sums[t, at, :]
                    change = ref[0, at, :].astype(jnp.float32) - before
                    sums[t, at, :] = before + to_column(share[g : g + 1], eye) * change

    for t in range(4):
        packed[d & 1, t, pl.ds(0, ROWS), :] = sums[t].astype(jnp.bfloat16)
        packed[d & 1, t, pl.ds(ROWS, 16), :] = lse_parts(lses[t, 0:4])
    copies = [pltpu.make_async_copy(packed.at[n % 2], outs[n], sem.at[n % 2]) for n in range(4)]
    for n in range(4):

        @pl.when(d == n)
        def _():
            copies[n].start()
            if n > 0:
                copies[n - 1].wait()
            if n == 3:
                copies[n].wait()


def merge_ring(h, codes, me, slots):
    return pl.pallas_call(
        functools.partial(ring_kernel, h),
        grid_spec=pltpu.PrefetchScalarGridSpec(
            num_scalar_prefetch=2,
            grid=(4,),
            in_specs=[pl.BlockSpec((2, 1, PAYLOAD, HD), lambda d, c, m: (0, d, 0, 0))] * 4,
            out_specs=[pl.BlockSpec(memory_space=pltpu.HBM)] * 4,
            scratch_shapes=[
                pltpu.VMEM((4, ROWS, HD), jnp.float32),
                pltpu.VMEM((4, 8, HD), jnp.float32),
                pltpu.VMEM((2, 4, PAYLOAD, HD), jnp.bfloat16),
                pltpu.SemaphoreType.DMA((2,)),
            ],
        ),
        out_shape=[pltpu.HBM((4, PAYLOAD, HD), jnp.bfloat16)] * 4,
        compiler_params=params(),
        cost_estimate=SMALL,
        name="ring",
    )(codes, me, *pinned(*slots))


def merge_kernel(own_ref, lse_ref, *refs):
    parts, o_ref = refs[:8], refs[8]
    eye = eye_mask()
    for h in range(2):
        arrived = parts[4 * h : 4 * h + 4]
        rows = [lse_ref[h, 0, 0:4, :]] + [lse_rows(ref[0, pl.ds(ROWS, 16), :]) for ref in arrived]
        top = functools.reduce(jnp.maximum, rows)
        weights = [jnp.exp2(x - top) for x in rows]
        total = functools.reduce(jnp.add, weights)
        weights = [w / total for w in weights]
        for g in range(GROUP):
            sums = [own_ref[h, 0, g]] + [ref[0, pl.ds(g * TILE, TILE), :].astype(jnp.float32) for ref in arrived]
            terms = [to_column(w[g : g + 1], eye) * (x - sums[0]) for w, x in zip(weights[1:], sums[1:])]
            at = (h * GROUP + g) * HD
            o_ref[0, :, at : at + HD] = functools.reduce(jnp.add, terms, sums[0]).astype(jnp.bfloat16)


def merge(lane, own, lse, parts):
    part = pl.BlockSpec((1, PAYLOAD, HD), lambda d, k: ((k[0] + d) & 3, 0, 0))
    return pl.pallas_call(
        lambda lane, *refs: merge_kernel(*refs),
        grid_spec=pltpu.PrefetchScalarGridSpec(
            num_scalar_prefetch=1,
            grid=(4,),
            in_specs=[
                pl.BlockSpec((2, 1, GROUP, TILE, HD), lambda d, k: (0, (k[0] + d) & 3, 0, 0, 0)),
                pl.BlockSpec((2, 1, 8, TILE), lambda d, k: (0, (k[0] + d) & 3, 0, 0)),
            ]
            + [part] * 8,
            out_specs=pl.BlockSpec((1, TILE, 2 * GROUP * HD), lambda d, k: (d, 0, 0)),
        ),
        out_shape=jax.ShapeDtypeStruct((4, TILE, 2 * GROUP * HD), jnp.bfloat16),
        compiler_params=params(),
        cost_estimate=SMALL,
        name="merge",
    )(lane, *pinned(own, lse, *parts[0], *parts[1]))


def own_projection_kernel(x_ref, w_ref, o_ref):
    o_ref[...] = jnp.dot(x_ref[...], w_ref[...], preferred_element_type=jnp.float32)


def own_projection(x, weights):
    columns = 1024
    return pl.pallas_call(
        own_projection_kernel,
        grid=(weights.shape[1] // columns,),
        in_specs=[
            pl.BlockSpec(x.shape, lambda j: (0, 0)),
            pl.BlockSpec((weights.shape[0], columns), lambda j: (0, j)),
        ],
        out_specs=pl.BlockSpec((TILE, columns), lambda j: (0, j)),
        out_shape=pltpu.HBM((TILE, weights.shape[1]), jnp.float32),
        compiler_params=params(),
        cost_estimate=SMALL,
        name="own_projection",
    )(x, weights)


def projection_kernel(lane, core, sum_ref, *refs):
    rows, mine, other, o_ref = refs[:3], refs[3:6], refs[6:9], refs[9]
    total = sum_ref[...]
    half = rows[0].shape[1] // 2
    at = pl.multiple_of(core[0] * half, half)
    away = pl.multiple_of((1 - core[0]) * half, half)
    for d in range(3):
        total += jnp.dot(rows[d][:, pl.ds(at, half)], mine[d][0], preferred_element_type=jnp.float32)
        total += jnp.dot(rows[d][:, pl.ds(away, half)], other[d][0], preferred_element_type=jnp.float32)
    o_ref[...] = total


def projection(lane, core, total, rows, mine, other):
    columns = 1024
    width = total.shape[1]

    def weight(d):
        return pl.BlockSpec((1, mine.shape[1], columns), lambda j, k, c: ((k[0] - d) & 3, 0, j))

    block = pl.BlockSpec((TILE, columns), lambda j, k, c: (0, j))
    return pl.pallas_call(
        projection_kernel,
        grid_spec=pltpu.PrefetchScalarGridSpec(
            num_scalar_prefetch=2,
            grid=(width // columns,),
            in_specs=[block]
            + [pl.BlockSpec(x.shape, lambda j, k, c: (0, 0)) for x in rows]
            + [weight(d) for d in (1, 2, 3)] * 2,
            out_specs=block,
        ),
        out_shape=jax.ShapeDtypeStruct(total.shape, jnp.float32),
        compiler_params=pltpu.CompilerParams(vmem_limit_bytes=2 * VMEM_LIMIT),
        cost_estimate=SMALL,
        name="projection",
    )(lane, core, *pinned(total, *rows), *([mine] * 3), *([other] * 3))


def shift(x, h, first, second, flip=0):
    pairs = [(i, moved(h, position(i), first, second, flip)) for i in range(32)]
    return lax.ppermute(x, "seq", pairs)


def tail_step(tail, step):
    if step == 0:
        pairs = [(device(3, 3, c), device(3, 0, c)) for c in range(2)]
    elif step == 1:
        pairs = [(device(3, a, c), device(3, b, c)) for a, b in ((3, 2), (0, 1)) for c in range(2)]
    elif step == 2:
        pairs = [(device(3, y, c), device(0, y, c)) for y in range(4) for c in range(2)]
    else:
        pairs = [(device(a, y, c), device(b, y, c)) for a, b in ((3, 2), (0, 1)) for y in range(4) for c in range(2)]
    return tail + lax.ppermute(tail, "seq", pairs)


def swap(x):
    return shift(x, 0, 0, 0, 1)


def all_to_all(x, axis):
    return lax.all_to_all(x, axis, split_axis=0, concat_axis=0, tiled=True)


def shards(queries, span_kv, cache, block_group, block_within, span_start, out_weight):
    seq_count = lax.axis_size("seq")
    me = lax.axis_index("seq")
    core = me & 1
    cache_len = cache.shape[1] * seq_count

    hits = block_group[:, None] == jnp.arange(seq_count, dtype=jnp.int32)[None, :, None, None]
    tiles = jnp.arange(4, dtype=jnp.int32)[None, None, :, None]
    code = jnp.sum(jnp.where(hits, block_within[:, None] + tiles * 16 + 1, 0), axis=(2, 3)) - 1
    codes = all_to_all(jnp.broadcast_to(code.reshape(1, -1), (seq_count, 2 * seq_count)), "seq").reshape(-1)
    place = me.reshape(1)

    barrier = lax.optimization_barrier
    own_tiles = split(queries)
    own_tiles, weights = barrier((own_tiles, out_weight))
    half = half_rows(core.reshape(1), weights)
    one = [shift(own_tiles[h], h, 1, 0) for h in range(2)]
    three = [shift(own_tiles[h], h, 3, 0) for h in range(2)]
    last = cache[:, -BLOCK:]
    tail = jnp.where(me == seq_count - 1, last[1], lax.ppermute(last[0], "seq", [(31, 30)]))
    tail = tail_step(tail, 0)
    codes, one, three, tail, half = barrier((codes, one, three, tail, half))
    mine = lax.all_gather(half, "kvh", axis=0, tiled=True)
    low = [shift(one[h][:2], h, 1, 0) for h in range(2)]
    high = [shift(three[h][2:], h, 3, 0) for h in range(2)]
    tail = tail_step(tail, 1)
    partner = swap(cache)
    low, high, tail, partner = barrier((low, high, tail, partner))

    def attend(e, arrays):
        return attend_slots(e, codes, place, arrays, (cache, partner))

    packed = pack(codes, place, [x for h in range(2) for x in (own_tiles[h], one[h], three[h], low[h], high[h])])
    near = [[shift(packed[h][e], h, 0, e) for h in range(2)] for e in (1, 3)]
    tail = tail_step(tail, 2)
    back0 = attend(0, [packed[h][0] for h in range(2)])
    far = [packed[h][2] for h in range(2)]
    near, far, tail, back0 = barrier((near, far, tail, back0))
    far = [shift(far[h], h, 0, 2) for h in range(2)]
    tail = tail_step(tail, 3)
    out1 = attend(1, near[0])
    out3 = attend(3, near[1])
    far, tail, out1, out3 = barrier((far, tail, out1, out3))
    back1 = [shift(out1[h], h, 0, -1) for h in range(2)]
    back3 = [shift(out3[h], h, 0, -3) for h in range(2)]
    out2 = attend(2, far)
    back1, back3, tail, out2 = barrier((back1, back3, tail, out2))
    back2 = [shift(out2[h], h, 0, -2) for h in range(2)]
    other = swap(tail)
    tail = jnp.where(core == 0, tail, other), jnp.where(core == 0, other, tail)
    own, lse = attend_local(span_start, queries, span_kv, tail, cache_len)
    back1, back3, back2, own, lse = barrier((back1, back3, back2, own, lse))

    rings = [merge_ring(h, codes, place, (back0[h], back1[h], back2[h], back3[h])) for h in range(2)]
    parts = [[rings[h][0]] + [shift(rings[h][d], h, -d, 0) for d in (1, 3, 2)] for h in range(2)]
    parts[0], mine = barrier((parts[0], mine))
    other = swap(mine)
    lane = lax.axis_index("kvh").reshape(1)
    attended = merge(lane, own, lse, parts)
    rows = []
    for d in (1, 2, 3):
        rows.append(lax.ppermute(attended[d], "kvh", [(k, (k + d) % 4) for k in range(4)]))
    total = own_projection(attended[0], out_weight)
    mine, other = mine.reshape(4, 512, -1), other.reshape(4, 512, -1)
    return projection(lane, core.reshape(1), total, rows, mine, other)


def solution(mesh):
    in_specs = (
        P("seq", "kvh"),
        P(None, "seq", "kvh"),
        P(None, "seq", "kvh"),
        P("kvh", "seq", None),
        P("kvh", "seq", None),
        P(),
        P("kvh", None),
    )
    out_specs = P(("seq", "kvh"), None)
    return jax.shard_map(shards, mesh=mesh, in_specs=in_specs, out_specs=out_specs, check_vma=False)
```
